256 devices in a mesh: lat: 16 (over z, x_hi), lon: 16 (over y, x_lo, core).
Axes of the slice: x: 4 (x_hi: 2, x_lo: 2; x = x_hi * 2 + x_lo), y: 4, z: 8, core: 2. Of those that a mesh axis runs over, the one named last changes fastest.
Arguments:
- features: bfloat16 [192, 720, 256], P('lat', 'lon'), may hold values from -6 to 6
- cotangent: bfloat16 [192, 720, 256], P('lat', 'lon'), may hold values from -6 to 6
- weights: bfloat16 [9, 256, 256], replicated, may hold values from -0.125 to 0.125
- quad_weights: bfloat16 [9, 192, 9, 17], replicated, may hold values from -0.71875 to 0.71875
- reach_table: int32 [192, 9], replicated, may hold values from 1 to 8
Outputs:
- grad_input: bfloat16 [192, 720, 256], P('lat', 'lon')
- grad_weight: float32 [9, 256, 256], replicated
The draws below stay inside these ranges and needn't reach their ends.
All inputs are finite; a program needn't handle non-finite values.
Results may differ from the reference program's by a relative error of at most 0.0065.
Values may be sent and summed in bfloat16 or wider, within the bound.
No kernel may reach another device: no remote copies, remote signals or barrier semaphores. Data moves between devices by JAX's collectives and lax.ppermute only.
A program may use at most 192 MiB of HBM per device.

```python
import math
import jax
import jax.numpy as jnp
from jax import lax

C_IN = 256
C_OUT = 256
BASIS = 9
RAD_LAT = 4
RAD_LON = 8
NLAT = 192
NLON = 720


def place_ends(result, own_key, least, largest):
    extent = result.shape
    index_at = [jax.random.randint(jax.random.fold_in(own_key, axis), (), 0, extent[axis]) for axis in range(len(extent))]
    result = result.at[tuple(index_at)].set(least)
    longest = extent.index(max(extent))
    index_at[longest] = (index_at[longest] + 1) % extent[longest]
    return result.at[tuple(index_at)].set(largest)


def steps_of(own_key, shape, split, least, top_value):
    level = 1.0
    for position, parts in split:
        steps = jax.random.uniform(jax.random.fold_in(jax.random.fold_in(own_key, 6), position), (parts,), jnp.float32, least / len(split), top_value / len(split))
        level = level * jnp.repeat(jnp.exp(steps), shape[position] // parts).reshape((-1,) + (1,) * (len(shape) - 1 - position))
    return level


def normal_values(own_key, shape, scale, reach, cuts=(), kind=jnp.bfloat16):
    loudness = steps_of(own_key, shape, cuts, -0.22, 0.18) if cuts else 1.0
    drawn = jax.random.normal(own_key, shape, jnp.float32) * scale * loudness
    return jnp.minimum(jnp.maximum(drawn, -reach), reach).astype(kind)


def setup_inputs(seed: int = 0) -> dict:
    keys = jax.random.split(jax.random.key(seed), 6)
    return {
        "features": normal_values(keys[0], (NLAT, NLON, C_IN), 1.0, 6.0, ((0, 16), (1, 16))),
        "cotangent": normal_values(keys[1], (NLAT, NLON, C_OUT), 1.0, 6.0, ((0, 16), (1, 16))),
        "weights": normal_values(keys[2], (BASIS, C_IN, C_OUT), (BASIS * C_IN) ** -0.5, 0.125),
        "quad_weights": normal_values(keys[3], (BASIS, NLAT, 2 * RAD_LAT + 1, 2 * RAD_LON + 1), 0.12, 0.71875),
        "reach_table": place_ends(jax.random.randint(keys[4], (NLAT, 2 * RAD_LAT + 1), 1, RAD_LON + 1), jax.random.fold_in(keys[4], 1), 1, RAD_LON).astype(jnp.int32),
    }


def reference(features, cotangent, weights, quad_weights, reach_table):
    n_lat, n_lon, chans = features.shape
    basis = quad_weights.shape[0]
    taps_lat = quad_weights.shape[2]
    taps_lon = quad_weights.shape[3]
    rad_lat = (taps_lat - 1) // 2
    rad_lon = (taps_lon - 1) // 2
    wide = jnp.concatenate([features[:, n_lon - rad_lon:], features, features[:, :rad_lon]], axis=1).astype(jnp.float32)
    padded = jnp.pad(wide, ((rad_lat, rad_lat), (0, 0), (0, 0)))
    weights_wide = weights.astype(jnp.float32)
    tap_ids = jnp.arange(taps_lon, dtype=jnp.int32)

    def step(carry, row):
        grad_w, spread = carry
        window = lax.dynamic_slice_in_dim(padded, row, taps_lat, 0)
        psi_row = lax.dynamic_index_in_dim(quad_weights, row, 1, keepdims=False).astype(jnp.float32)
        reach_row = lax.dynamic_index_in_dim(reach_table, row, 0, keepdims=False)
        keep = (jnp.abs(tap_ids[None, :] - rad_lon) <= reach_row[:, None]).astype(jnp.float32)
        psi_row = psi_row * keep[None]
        out_row = jnp.zeros((basis, n_lon, chans), jnp.float32)
        for tap in range(taps_lon):
            out_row = out_row + jnp.einsum('ka,ajc->kjc', psi_row[:, :, tap], window[:, tap:tap + n_lon])
        z_row = lax.optimization_barrier(out_row.astype(jnp.bfloat16)).astype(jnp.float32)
        cot_row = lax.dynamic_index_in_dim(cotangent, row, 0, keepdims=False).astype(jnp.float32)
        grad_w = grad_w + jnp.einsum('kjc,jo->kco', z_row, cot_row)
        mixed = jnp.einsum('jo,kco->kjc', cot_row, weights_wide)
        u_row = lax.optimization_barrier(mixed.astype(jnp.bfloat16)).astype(jnp.float32)
        contrib = jnp.zeros((taps_lat, n_lon + 2 * rad_lon, chans), jnp.float32)
        for tap in range(taps_lon):
            contrib = contrib.at[:, tap:tap + n_lon].add(jnp.einsum('ka,kjc->ajc', psi_row[:, :, tap], u_row))
        current = lax.dynamic_slice_in_dim(spread, row, taps_lat, 0)
        spread = lax.dynamic_update_slice_in_dim(spread, current + contrib, row, 0)
        return ((grad_w, spread), None)
    init = (jnp.zeros((basis, chans, cotangent.shape[2]), jnp.float32), jnp.zeros((n_lat + 2 * rad_lat, n_lon + 2 * rad_lon, chans), jnp.float32))
    rows = jnp.arange(n_lat, dtype=jnp.int32)
    (grad_w, spread), _ = lax.scan(step, init, rows)
    core = spread[rad_lat:rad_lat + n_lat]
    middle = core[:, rad_lon:rad_lon + n_lon]
    middle = middle.at[:, n_lon - rad_lon:].add(core[:, :rad_lon])
    middle = middle.at[:, :rad_lon].add(core[:, n_lon + rad_lon:])
    scale = 1.0 / math.sqrt(n_lat * n_lon)
    return (middle.astype(jnp.bfloat16), grad_w * scale)
```

```python
import math

import jax
import jax.numpy as jnp
from jax import lax
from jax.experimental import pallas as pl
from jax.experimental.pallas import tpu as pltpu
from jax.sharding import PartitionSpec as P

F32 = jnp.float32
BF16 = jnp.bfloat16
BOTH = ("lat", "lon")
WIDE = 48
WIN = 32
SPAN = 12


def coords(index):
    lat, lon = divmod(index, 16)
    return {"z": lat // 2, "x": lat % 2 * 2 + lon // 2 % 2, "y": lon // 4, "c": lon % 2}


def index_of(at):
    return (at["z"] * 2 + at["x"] // 2) * 16 + at["y"] * 4 + at["x"] % 2 * 2 + at["c"]


def route(**moves):
    pairs = []
    for source in range(256):
        at = coords(source)
        for axis, move in moves.items():
            at[axis] = move(at[axis])
        pairs.append((source, index_of(at)))
    return pairs


def flip(v):
    return v ^ 1


def mirror(v):
    return 3 - v


CORE = route(c=flip)
SQUARE0 = [route(x=flip), route(y=flip), route(x=flip, y=flip)]
SQUARE1 = [route(x=mirror), route(y=mirror), route(x=mirror, y=mirror)]
ZS = [route(z=flip), route(z=lambda v: v ^ 2), route(z=lambda v: 7 - v)]


def send(value, pairs):
    return lax.ppermute(value, BOTH, pairs)


def whole(n):
    return [pl.BlockSpec(memory_space=pltpu.VMEM)] * n


SMEM = pl.BlockSpec(memory_space=pltpu.SMEM)
PARAMS = pltpu.CompilerParams(vmem_limit_bytes=40 * 1024 * 1024)


def band_kernel(base_ref, band_ref):
    def pair(u, _):
        for pp in range(2):
            for k in range(9):
                line = jnp.broadcast_to(base_ref[2 * u + pp, pl.ds(k, 1), :], (16, SPAN * WIN))
                line = pltpu.roll(line, pp * WIN, 1, stride=1, stride_axis=0)
                first = (pp * 9 + k) * 16
                band_ref[u, first : first + 16, :] = line.astype(BF16)
        return 0

    lax.fori_loop(0, 6, pair, 0)


def grad_kernel(core_ref, ext_ref, band_ref, feat_ref, y_ref, keep_ref, send_ref):
    def pair(u, _):
        band = band_ref[u]
        for t in range(3):
            window = ext_ref[pl.ds(2 * u, SPAN), 16 * t : 16 * t + WIN, :].reshape(SPAN * WIN, 256)
            rows = jnp.dot(band, window, preferred_element_type=F32).astype(BF16)
            for pp in range(2):
                for k in range(9):
                    start = pl.multiple_of((2 * u + pp) * WIDE + 16 * t, 16)
                    first = (pp * 9 + k) * 16
                    y_ref[k, pl.ds(start, 16), :] = rows[first : first + 16]
        return 0

    lax.fori_loop(0, 6, pair, 0)
    core = core_ref[0]
    own = pl.multiple_of(core * 128, 128)
    other = pl.multiple_of(128 - core * 128, 128)
    feat = jnp.concatenate([feat_ref[pl.ds(own, 128), :], feat_ref[pl.ds(other, 128), :]], axis=0)
    for k in range(9):
        part = jnp.dot(feat, y_ref[k], preferred_element_type=F32)
        keep_ref[k] = part[:128]
        send_ref[k] = part[128:].astype(BF16)


def input_kernel(y_ref, w_ref, out_ref):
    total = jnp.zeros((12 * WIDE, 256), F32)
    for k in range(9):
        total += lax.dot_general(
            y_ref[k], w_ref[k], (((1,), (1,)), ((), ())), preferred_element_type=F32
        )
    total = total.reshape(12, WIDE, 256)
    out_ref[...] = total[:, :45].astype(BF16)


def split0_kernel(at_ref, keep_ref, got_ref, own_ref, *send_refs):
    here = at_ref[0]
    for m, ref in enumerate((own_ref,) + send_refs):
        start = pl.multiple_of((here ^ m) * 32, 32)
        rows = pl.ds(start, 32)
        part = keep_ref[:, rows, :] + got_ref[:, rows, :].astype(F32)
        ref[...] = part.astype(ref.dtype)


def split1_kernel(at_ref, keep_ref, got1, got2, got3, own_ref, *send_refs):
    here = at_ref[0]
    for m, ref in enumerate((own_ref,) + send_refs):
        block = here ^ m
        rows = pl.ds(pl.multiple_of((block // 2) * 16, 16), 16)
        cols = pl.ds(pl.multiple_of((block % 2) * 128, 128), 128)
        part = keep_ref[:, rows, cols]
        for got in (got1, got2, got3):
            part = part + got[:, rows, cols].astype(F32)
        ref[...] = part.astype(ref.dtype)


def join_kernel(scale, at_ref, own_ref, got_ref, out_ref):
    core, block0, block1 = at_ref[0], at_ref[1], at_ref[2]
    for j, ref in enumerate((own_ref, got_ref)):
        for m0 in range(4):
            for m1 in range(4):
                piece = block1 ^ m1
                start = (core ^ j) * 128 + (block0 ^ m0) * 32 + (piece // 2) * 16
                rows = pl.ds(pl.multiple_of(start, 16), 16)
                cols = pl.ds(pl.multiple_of((piece % 2) * 128, 128), 128)
                out_ref[:, rows, cols] = ref[4 * m0 + m1].astype(F32) * scale


def call(kernel, outs, specs, *args, **cost):
    estimate = pl.CostEstimate(transcendentals=0, **cost) if cost else None
    return pl.pallas_call(
        kernel,
        out_shape=outs,
        in_specs=specs,
        out_specs=jax.tree.map(lambda _: pl.BlockSpec(memory_space=pltpu.VMEM), outs),
        compiler_params=PARAMS,
        cost_estimate=estimate,
    )(*args)


def shape(dims, dtype):
    return jax.ShapeDtypeStruct(dims, dtype)


def halo(block, axis, dim, width, periodic):
    count = lax.axis_size(axis)
    forward = [(i, i + 1) for i in range(count - 1)]
    if periodic:
        forward.append((count - 1, 0))
    backward = [(target, source) for source, target in forward]
    high = block.shape[dim]
    low = lax.ppermute(lax.slice_in_dim(block, high - width, high, axis=dim), axis, forward)
    return low, lax.ppermute(lax.slice_in_dim(block, 0, width, axis=dim), axis, backward)


def band_base(quad_weights, reach_table):
    first = lax.axis_index("lat") * 12 - 4
    start = jnp.clip(first, 0, 192 - 20)
    psi = lax.dynamic_slice_in_dim(quad_weights, start, 20, 1)
    reach = lax.dynamic_slice_in_dim(reach_table, start, 20, 0)
    taps = lax.broadcasted_iota(jnp.int32, (1, 1, 1, 17), 3)
    psi = jnp.where(jnp.abs(taps - 8) <= reach[None, :, :, None], psi, jnp.zeros_like(psi))
    psi = jnp.pad(psi, ((0, 0), (4, 4), (0, 0), (0, 0)))
    psi = lax.dynamic_slice_in_dim(psi, first - start + 4, 20, 1)
    psi = jnp.pad(psi[..., ::-1], ((0, 0), (0, 0), (0, 0), (0, WIN - 17))).astype(F32)
    psi = psi.transpose(1, 0, 2, 3)
    rows = [psi[er : er + 12, :, 8 - er] for er in range(9)]
    rows.append(jnp.zeros((12, 9, (SPAN - 9) * WIN), F32))
    return jnp.concatenate(rows, axis=2)


def local(features, cotangent, weights, quad_weights, reach_table):
    lat, lon = lax.axis_index("lat"), lax.axis_index("lon")
    x, y, core = (lat % 2) * 2 + (lon // 2) % 2, lon // 4, lon % 2
    block0 = ((x + 1) // 2) % 2 + 2 * (((y + 1) // 2) % 2)
    block1 = x // 2 + 2 * (y // 2)

    above, below = halo(cotangent, "lat", 0, 4, False)
    base = band_base(quad_weights, reach_table)
    feat = jnp.pad(features, ((0, 0), (0, WIDE - 45), (0, 0))).reshape(12 * WIDE, 256).T
    band = call(band_kernel, shape((6, 288, SPAN * WIN), BF16), whole(1), base)
    tall = jnp.concatenate([above, cotangent, below], axis=0)
    left, right = halo(tall, "lon", 1, 8, True)
    ext = jnp.concatenate([left, tall, right], axis=1)
    ext = jnp.pad(ext, ((0, 2), (0, 3), (0, 0)))

    halves = (9, 128, 256)
    y_all, keep, out = call(
        grad_kernel,
        (shape((9, 12 * WIDE, 256), BF16), shape(halves, F32), shape(halves, BF16)),
        [SMEM] + whole(3),
        core[None], ext, band, feat,
        flops=6 * 10**9, bytes_accessed=8 * 10**6,
    )
    got = send(out, CORE)
    part = (9, 32, 256)
    keep, *outs = call(
        split0_kernel, (shape(part, F32),) + (shape(part, BF16),) * 3, [SMEM] + whole(2),
        block0[None], keep, got,
    )
    gots = [send(v, r) for v, r in zip(outs, SQUARE0)]
    grad_input = call(
        input_kernel, shape((12, 45, 256), BF16), whole(2), y_all, weights,
        flops=2 * 10**9, bytes_accessed=4 * 10**6,
    )
    part = (9, 16, 128)
    keep, *outs = call(
        split1_kernel, (shape(part, F32),) + (shape(part, BF16),) * 3, [SMEM] + whole(4),
        block1[None], keep, *gots,
    )
    total = keep
    for v, r in zip(outs, SQUARE1):
        total = total + send(v, r).astype(F32)
    for r in ZS:
        mine = total.astype(BF16)
        total = mine.astype(F32) + send(mine, r).astype(F32)
    mine = total.astype(BF16)
    mine = jnp.stack([mine] + [send(mine, r) for r in SQUARE1])
    mine = jnp.concatenate([mine] + [send(mine, r) for r in SQUARE0])
    got = send(mine, CORE)
    scale = 1.0 / math.sqrt(192 * 720)
    grad_weight = call(
        lambda *refs: join_kernel(scale, *refs), shape((9, 256, 256), F32), [SMEM] + whole(2),
        jnp.stack([core, block0, block1]), mine, got,
    )
    return grad_input, grad_weight


def solution(mesh):
    return jax.shard_map(
        local,
        mesh=mesh,
        in_specs=(P("lat", "lon", None), P("lat", "lon", None), P(), P(), P()),
        out_specs=(P("lat", "lon", None), P()),
        check_vma=False,
    )
```

```python
import functools
import math

import jax
import jax.numpy as jnp
from jax import lax
from jax.experimental import pallas as pl
from jax.experimental.pallas import tpu as pltpu
from jax.sharding import PartitionSpec as P

F32 = jnp.float32
BF16 = jnp.bfloat16
BOTH = ("lat", "lon")
WIDE = 48
WIN = 32
SPAN = 12


def coords(index):
    lat, lon = divmod(index, 16)
    return {"z": lat // 2, "x": lat % 2 * 2 + lon // 2 % 2, "y": lon // 4, "c": lon % 2}


def index_of(at):
    return (at["z"] * 2 + at["x"] // 2) * 16 + at["y"] * 4 + at["x"] % 2 * 2 + at["c"]


def route(**moves):
    pairs = []
    for source in range(256):
        at = coords(source)
        for axis, move in moves.items():
            at[axis] = move(at[axis])
        pairs.append((source, index_of(at)))
    return pairs


def flip(v):
    return v ^ 1


CORE = route(c=flip)
PLANES = [
    [i for i in range(256) if coords(i)["z"] == z and coords(i)["c"] == c]
    for z in range(8)
    for c in range(2)
]
ZS = [route(z=flip), route(z=lambda v: v ^ 2), route(z=lambda v: 7 - v)]


def send(value, pairs):
    return lax.ppermute(value, BOTH, pairs)


def trade(blocks):
    return lax.all_to_all(blocks, BOTH, 0, 0, axis_index_groups=PLANES, tiled=True)


def whole(n):
    return [pl.BlockSpec(memory_space=pltpu.VMEM)] * n


SMEM = pl.BlockSpec(memory_space=pltpu.SMEM)
ANY = pl.BlockSpec(memory_space=pl.ANY)
PARAMS = pltpu.CompilerParams(vmem_limit_bytes=16 * 1024 * 1024)


def band_kernel(base_ref, feat_ref, band_ref, out_ref, wide_ref):
    wide_ref[...] = jnp.zeros_like(wide_ref)
    wide_ref[:, :45, :] = feat_ref[...]
    out_ref[...] = wide_ref[...].reshape(12 * WIDE, 256).T

    def pair(u, _):
        for pp in range(2):
            for k in range(9):
                line = jnp.broadcast_to(base_ref[2 * u + pp, pl.ds(k, 1), :], (16, SPAN * WIN))
                line = pltpu.roll(line, pp * WIN, 1, stride=1, stride_axis=0)
                first = (pp * 9 + k) * 16
                band_ref[u, first : first + 16, :] = line.astype(BF16)
        return 0

    lax.fori_loop(0, 6, pair, 0)


def grad_kernel(core_ref, ext_ref, band_ref, feat_ref, y_ref, keep_ref, send_ref):
    def pair(u, _):
        band = band_ref[u]
        for t in range(3):
            window = ext_ref[pl.ds(2 * u, SPAN), 16 * t : 16 * t + WIN, :].reshape(SPAN * WIN, 256)
            rows = jnp.dot(band, window, preferred_element_type=F32).astype(BF16)
            for pp in range(2):
                for k in range(9):
                    start = pl.multiple_of((2 * u + pp) * WIDE + 16 * t, 16)
                    first = (pp * 9 + k) * 16
                    y_ref[k, pl.ds(start, 16), :] = rows[first : first + 16]
        return 0

    lax.fori_loop(0, 6, pair, 0)
    core = core_ref[0]
    own = pl.multiple_of(core * 128, 128)
    other = pl.multiple_of(128 - core * 128, 128)
    feat = jnp.concatenate([feat_ref[pl.ds(own, 128), :], feat_ref[pl.ds(other, 128), :]], axis=0)
    for k in range(9):
        part = jnp.dot(feat, y_ref[k], preferred_element_type=F32)
        keep_ref[k] = part[:128]
        send_ref[k] = part[128:].astype(BF16)


def input_kernel(y_ref, w_ref, out_ref):
    total = jnp.zeros((12 * WIDE, 256), F32)
    for k in range(9):
        total += lax.dot_general(
            y_ref[k], w_ref[k], (((1,), (1,)), ((), ())), preferred_element_type=F32
        )
    total = total.reshape(12, WIDE, 256)
    out_ref[...] = total[:, :45].astype(BF16)


def split_kernel(keep_ref, got_ref, out_ref):
    for j in range(16):
        rows, cols = slice(j // 2 * 16, j // 2 * 16 + 16), slice(j % 2 * 128, j % 2 * 128 + 128)
        part = keep_ref[:, rows, cols] + got_ref[:, rows, cols].astype(F32)
        out_ref[j] = part.astype(BF16)


def sum_kernel(got_ref, out_ref):
    total = got_ref[0].astype(F32)
    for j in range(1, 16):
        total = total + got_ref[j].astype(F32)
    out_ref[...] = total.astype(BF16)


def join_kernel(scale, other, core_ref, blocks_ref, *refs):
    out_ref, half_ref, sem = refs[-3:]
    half = core_ref[0] ^ other
    start = pl.multiple_of(half * 128, 128)
    for j in range(16):
        rows, cols = slice(j // 2 * 16, j // 2 * 16 + 16), slice(j % 2 * 128, j % 2 * 128 + 128)
        half_ref[:, rows, cols] = blocks_ref[j].astype(F32) * scale
    copy = pltpu.make_async_copy(half_ref, out_ref.at[:, pl.ds(start, 128), :], sem)
    copy.start()
    copy.wait()


def call(kernel, outs, specs, *args, out_spec=None, scratch=(), aliases=None, **cost):
    estimate = pl.CostEstimate(transcendentals=0, **cost) if cost else None
    out_spec = out_spec or pl.BlockSpec(memory_space=pltpu.VMEM)
    return pl.pallas_call(
        kernel,
        out_shape=outs,
        in_specs=specs,
        out_specs=jax.tree.map(lambda _: out_spec, outs),
        scratch_shapes=scratch,
        input_output_aliases=aliases or {},
        compiler_params=PARAMS,
        cost_estimate=estimate,
    )(*args)


def shape(dims, dtype):
    return jax.ShapeDtypeStruct(dims, dtype)


def halo(block, axis, dim, width, periodic):
    count = lax.axis_size(axis)
    forward = [(i, i + 1) for i in range(count - 1)]
    if periodic:
        forward.append((count - 1, 0))
    backward = [(target, source) for source, target in forward]
    high = block.shape[dim]
    low = lax.ppermute(lax.slice_in_dim(block, high - width, high, axis=dim), axis, forward)
    return low, lax.ppermute(lax.slice_in_dim(block, 0, width, axis=dim), axis, backward)


def band_base(quad_weights, reach_table):
    first = lax.axis_index("lat") * 12 - 4
    start = jnp.clip(first, 0, 192 - 20)
    psi = lax.dynamic_slice_in_dim(quad_weights, start, 20, 1)
    reach = lax.dynamic_slice_in_dim(reach_table, start, 20, 0)
    taps = lax.broadcasted_iota(jnp.int32, (1, 1, 1, 17), 3)
    psi = jnp.where(jnp.abs(taps - 8) <= reach[None, :, :, None], psi, jnp.zeros_like(psi))
    psi = jnp.pad(psi, ((0, 0), (4, 4), (0, 0), (0, 0)))
    psi = lax.dynamic_slice_in_dim(psi, first - start + 4, 20, 1)
    psi = jnp.pad(psi[..., ::-1], ((0, 0), (0, 0), (0, 0), (0, WIN - 17))).astype(F32)
    psi = psi.transpose(1, 0, 2, 3)
    rows = [psi[er : er + 12, :, 8 - er] for er in range(9)]
    rows.append(jnp.zeros((12, 9, (SPAN - 9) * WIN), F32))
    return jnp.concatenate(rows, axis=2)


def local(features, cotangent, weights, quad_weights, reach_table):
    core = (lax.axis_index("lon") % 2)[None]

    above, below = halo(cotangent, "lat", 0, 4, False)
    base = band_base(quad_weights, reach_table)
    band, feat = call(
        band_kernel, (shape((6, 288, SPAN * WIN), BF16), shape((256, 12 * WIDE), BF16)), whole(2),
        base, features, scratch=[pltpu.VMEM((12, WIDE, 256), BF16)],
    )
    tall = jnp.concatenate([above, cotangent, below], axis=0)
    left, right = halo(tall, "lon", 1, 8, True)
    ext = jnp.concatenate([left, tall, right], axis=1)
    ext = jnp.pad(ext, ((0, 2), (0, 3), (0, 0)))

    halves, blocks = (9, 128, 256), (16, 9, 16, 128)
    y_all, keep, out = call(
        grad_kernel,
        (shape((9, 12 * WIDE, 256), BF16), shape(halves, F32), shape(halves, BF16)),
        [SMEM] + whole(3), core, ext, band, feat,
        flops=6 * 10**9, bytes_accessed=8 * 10**6,
    )
    got = send(out, CORE)
    got = trade(call(split_kernel, shape(blocks, BF16), whole(2), keep, got))
    mine = call(sum_kernel, shape(blocks[1:], BF16), whole(1), got)
    total = mine.astype(F32) + send(mine, ZS[0]).astype(F32)
    mine, y_all = lax.optimization_barrier((total.astype(BF16), y_all))
    got = send(mine, ZS[1])
    grad_input = call(
        input_kernel, shape((12, 45, 256), BF16), whole(2), y_all, weights,
        flops=2 * 10**9, bytes_accessed=4 * 10**6,
    )
    total = mine.astype(F32) + got.astype(F32)
    mine, grad_input = lax.optimization_barrier((total.astype(BF16), grad_input))
    total = mine.astype(F32) + send(mine, ZS[2]).astype(F32)
    own = trade(jnp.broadcast_to(total.astype(BF16), blocks))
    got = send(own, CORE)
    scale = 1.0 / math.sqrt(192 * 720)
    scratch = [pltpu.VMEM(halves, F32), pltpu.SemaphoreType.DMA]
    full = shape((9, 256, 256), F32)
    grad_weight = call(
        functools.partial(join_kernel, scale, 0), full, [SMEM] + whole(1), core, own,
        out_spec=ANY, scratch=scratch, flops=10**6, bytes_accessed=2 * 10**6,
    )
    grad_weight = call(
        functools.partial(join_kernel, scale, 1), full, [SMEM] + whole(1) + [ANY], core, got, grad_weight,
        out_spec=ANY, scratch=scratch, aliases={2: 0}, flops=10**6, bytes_accessed=2 * 10**6,
    )
    return grad_input, grad_weight


def solution(mesh):
    return jax.shard_map(
        local,
        mesh=mesh,
        in_specs=(P("lat", "lon", None), P("lat", "lon", None), P(), P(), P()),
        out_specs=(P("lat", "lon", None), P()),
        check_vma=False,
    )
```

```python
import functools
import math

import jax
import jax.numpy as jnp
from jax import lax
from jax.experimental import pallas as pl
from jax.experimental.pallas import tpu as pltpu
from jax.sharding import PartitionSpec as P

F32 = jnp.float32
BF16 = jnp.bfloat16
BOTH = ("lat", "lon")
WIDE = 48
WIN = 32


def coords(index):
    lat, lon = divmod(index, 16)
    return {"z": lat // 2, "x": lat % 2 * 2 + lon // 2 % 2, "y": lon // 4, "c": lon % 2}


def index_of(at):
    return (at["z"] * 2 + at["x"] // 2) * 16 + at["y"] * 4 + at["x"] % 2 * 2 + at["c"]


def route(**moves):
    pairs = []
    for source in range(256):
        at = coords(source)
        for axis, move in moves.items():
            at[axis] = move(at[axis])
        pairs.append((source, index_of(at)))
    return pairs


def flip(v):
    return v ^ 1


CORE = route(c=flip)
PLANES = [
    [i for i in range(256) if coords(i)["z"] == z and coords(i)["c"] == c]
    for z in range(8)
    for c in range(2)
]
ZS = [route(z=flip), route(z=lambda v: v ^ 2), route(z=lambda v: 7 - v)]


def send(value, pairs):
    return lax.ppermute(value, BOTH, pairs)


def trade(blocks):
    return lax.all_to_all(blocks, BOTH, 0, 0, axis_index_groups=PLANES, tiled=True)


def whole(n):
    return [pl.BlockSpec(memory_space=pltpu.VMEM)] * n


SMEM = pl.BlockSpec(memory_space=pltpu.SMEM)
ANY = pl.BlockSpec(memory_space=pl.ANY)
PARAMS = pltpu.CompilerParams(vmem_limit_bytes=16 * 1024 * 1024)


def groups(u):
    return max(0, 2 * u - 8) // 4, min(11, 2 * u + 1) // 4


def band_kernel(base_ref, feat_ref, band_ref, out_ref, wide_ref):
    wide_ref[...] = jnp.zeros_like(wide_ref)
    wide_ref[:, :45, :] = feat_ref[...]
    out_ref[...] = wide_ref[...].reshape(12 * WIDE, 256).T
    for u in range(10):
        low, high = groups(u)
        for pp in range(2):
            for k in range(9):
                first = (pp * 9 + k) * 16
                for g in range(low, high + 1):
                    lanes = slice(128 * g, 128 * g + 128)
                    line = jnp.broadcast_to(base_ref[2 * u + pp, k : k + 1, lanes], (16, 128))
                    line = pltpu.roll(line, 0, 1, stride=1, stride_axis=0)
                    band_ref[u, first : first + 16, lanes] = line.astype(BF16)


def halves_of(core, ref):
    own = pl.multiple_of(core * 128, 128)
    other = pl.multiple_of(128 - core * 128, 128)
    return jnp.concatenate([ref[pl.ds(own, 128), :], ref[pl.ds(other, 128), :]], axis=0)


def spread_kernel(core_ref, ext_ref, band_ref, feat_ref, y_ref, part_ref):
    for u in range(10):
        low, high = groups(u)
        band = band_ref[u, :, 128 * low : 128 * high + 128]
        for t in range(3):
            window = ext_ref[4 * low : 4 * high + 4, 16 * t : 16 * t + WIN, :].reshape(-1, 256)
            rows = jnp.dot(band, window, preferred_element_type=F32).astype(BF16)
            for pp in range(2):
                start = (2 * u + pp) * WIDE + 16 * t
                for k in range(9):
                    first = (pp * 9 + k) * 16
                    y_ref[k, start : start + 16, :] = rows[first : first + 16]
    feat = halves_of(core_ref[0], feat_ref)
    for k in range(9):
        part_ref[k] = jnp.dot(feat, y_ref[k, 4 * WIDE : 16 * WIDE], preferred_element_type=F32)


def edge_kernel(core_ref, part_ref, y_ref, above_ref, below_ref, keep_ref, send_ref, wide_ref, turned_ref):
    wide_ref[...] = jnp.zeros_like(wide_ref)
    wide_ref[:4, :45, :] = above_ref[...]
    wide_ref[4:, :45, :] = below_ref[...]
    turned_ref[...] = wide_ref[...].reshape(8 * WIDE, 256).T
    feat = halves_of(core_ref[0], turned_ref)
    for k in range(9):
        y = jnp.concatenate([y_ref[k, : 4 * WIDE], y_ref[k, 16 * WIDE :]], axis=0)
        part = part_ref[k] + jnp.dot(feat, y, preferred_element_type=F32)
        keep_ref[k] = part[:128]
        send_ref[k] = part[128:].astype(BF16)


def input_kernel(y_ref, w_ref, top_ref, middle_ref, bottom_ref):
    total = jnp.zeros((20 * WIDE, 256), F32)
    for k in range(9):
        total += lax.dot_general(
            y_ref[k], w_ref[k], (((1,), (1,)), ((), ())), preferred_element_type=F32
        )
    total = total.reshape(20, WIDE, 256)[:, :45]
    top_ref[...] = total[:4].astype(BF16)
    middle_ref[...] = total[4:16]
    bottom_ref[...] = total[16:].astype(BF16)


def fold_kernel(middle_ref, first_ref, last_ref, out_ref):
    out_ref[:4] = (middle_ref[:4] + first_ref[...].astype(F32)).astype(BF16)
    out_ref[4:8] = middle_ref[4:8].astype(BF16)
    out_ref[8:] = (middle_ref[8:] + last_ref[...].astype(F32)).astype(BF16)


def split_kernel(keep_ref, got_ref, out_ref):
    for j in range(16):
        rows, cols = slice(j // 2 * 16, j // 2 * 16 + 16), slice(j % 2 * 128, j % 2 * 128 + 128)
        part = keep_ref[:, rows, cols] + got_ref[:, rows, cols].astype(F32)
        out_ref[j] = part.astype(BF16)


def sum_kernel(got_ref, out_ref):
    total = got_ref[0].astype(F32)
    for j in range(1, 16):
        total = total + got_ref[j].astype(F32)
    out_ref[...] = total.astype(BF16)


def join_kernel(scale, other, core_ref, blocks_ref, *refs):
    out_ref, half_ref, sem = refs[-3:]
    half = core_ref[0] ^ other
    start = pl.multiple_of(half * 128, 128)
    for j in range(16):
        rows, cols = slice(j // 2 * 16, j // 2 * 16 + 16), slice(j % 2 * 128, j % 2 * 128 + 128)
        half_ref[:, rows, cols] = blocks_ref[j].astype(F32) * scale
    copy = pltpu.make_async_copy(half_ref, out_ref.at[:, pl.ds(start, 128), :], sem)
    copy.start()
    copy.wait()


def call(kernel, outs, specs, *args, out_spec=None, scratch=(), aliases=None, **cost):
    estimate = pl.CostEstimate(transcendentals=0, **cost) if cost else None
    out_spec = out_spec or pl.BlockSpec(memory_space=pltpu.VMEM)
    return pl.pallas_call(
        kernel,
        out_shape=outs,
        in_specs=specs,
        out_specs=jax.tree.map(lambda _: out_spec, outs),
        scratch_shapes=scratch,
        input_output_aliases=aliases or {},
        compiler_params=PARAMS,
        cost_estimate=estimate,
    )(*args)


def shape(dims, dtype):
    return jax.ShapeDtypeStruct(dims, dtype)


def neighbours(axis, periodic):
    count = lax.axis_size(axis)
    forward = [(i, i + 1) for i in range(count - 1)]
    if periodic:
        forward.append((count - 1, 0))
    return forward, [(target, source) for source, target in forward]


def band_base(quad_weights, reach_table):
    first = lax.axis_index("lat") * 12
    psi = lax.dynamic_slice_in_dim(quad_weights, first, 12, 1)
    reach = lax.dynamic_slice_in_dim(reach_table, first, 12, 0)
    taps = lax.broadcasted_iota(jnp.int32, (1, 1, 1, 17), 3)
    psi = jnp.where(jnp.abs(taps - 8) <= reach[None, :, :, None], psi, jnp.zeros_like(psi))
    psi = jnp.pad(psi[..., ::-1], ((0, 0), (0, 0), (0, 0), (0, WIN - 17))).astype(F32)
    psi = psi.transpose(1, 2, 0, 3)
    rows = [jnp.pad(psi[i], ((i, 11 - i), (0, 0), (0, 0))) for i in range(12)]
    return jnp.concatenate(rows, axis=2)


def local(features, cotangent, weights, quad_weights, reach_table):
    core = (lax.axis_index("lon") % 2)[None]
    down, up = neighbours("lat", False)
    east, west = neighbours("lon", True)

    above = lax.ppermute(features[8:], "lat", down)
    below = lax.ppermute(features[:4], "lat", up)
    left = lax.ppermute(cotangent[:, 37:], "lon", east)
    right = lax.ppermute(cotangent[:, :8], "lon", west)
    base = band_base(quad_weights, reach_table)
    band, feat = call(
        band_kernel, (shape((10, 288, 12 * WIN), BF16), shape((256, 12 * WIDE), BF16)), whole(2),
        base, features, scratch=[pltpu.VMEM((12, WIDE, 256), BF16)],
    )
    ext = jnp.pad(jnp.concatenate([left, cotangent, right], axis=1), ((0, 0), (0, 3), (0, 0)))

    halves, blocks = (9, 128, 256), (16, 9, 16, 128)
    y_all, part = call(
        spread_kernel, (shape((9, 20 * WIDE, 256), BF16), shape((9, 256, 256), F32)),
        [SMEM] + whole(3), core, ext, band, feat, flops=6 * 10**9, bytes_accessed=8 * 10**6,
    )
    edge = shape((4, 45, 256), BF16)
    top, middle, bottom = call(
        input_kernel, (edge, shape((12, 45, 256), F32), edge), whole(2), y_all, weights,
        flops=2 * 10**9, bytes_accessed=4 * 10**6,
    )
    above, below, middle = lax.optimization_barrier((above, below, middle))
    keep, out = call(
        edge_kernel, (shape(halves, F32), shape(halves, BF16)), [SMEM] + whole(4),
        core, part, y_all, above, below,
        scratch=[pltpu.VMEM((8, WIDE, 256), BF16), pltpu.VMEM((256, 8 * WIDE), BF16)],
        flops=2 * 10**9, bytes_accessed=8 * 10**6,
    )
    got = send(out, CORE)
    got = trade(call(split_kernel, shape(blocks, BF16), whole(2), keep, got))
    mine = call(sum_kernel, shape(blocks[1:], BF16), whole(1), got)
    mine, top, bottom = lax.optimization_barrier((mine, top, bottom))
    got = send(mine, ZS[0])
    last = lax.ppermute(top, "lat", up)
    first = lax.ppermute(bottom, "lat", down)
    total = mine.astype(F32) + got.astype(F32)
    mine = total.astype(BF16)
    total = mine.astype(F32) + send(mine, ZS[1]).astype(F32)
    mine = total.astype(BF16)
    total = mine.astype(F32) + send(mine, ZS[2]).astype(F32)
    own = trade(jnp.broadcast_to(total.astype(BF16), blocks))
    own, first, last = lax.optimization_barrier((own, first, last))
    got = send(own, CORE)
    grad_input = call(fold_kernel, shape((12, 45, 256), BF16), whole(3), middle, first, last)
    scale = 1.0 / math.sqrt(192 * 720)
    scratch = [pltpu.VMEM(halves, F32), pltpu.SemaphoreType.DMA]
    full = shape((9, 256, 256), F32)
    grad_weight = call(
        functools.partial(join_kernel, scale, 0), full, [SMEM] + whole(1), core, own,
        out_spec=ANY, scratch=scratch, flops=10**6, bytes_accessed=2 * 10**6,
    )
    grad_weight = call(
        functools.partial(join_kernel, scale, 1), full, [SMEM] + whole(1) + [ANY], core, got, grad_weight,
        out_spec=ANY, scratch=scratch, aliases={2: 0}, flops=10**6, bytes_accessed=2 * 10**6,
    )
    return grad_input, grad_weight


def solution(mesh):
    return jax.shard_map(
        local,
        mesh=mesh,
        in_specs=(P("lat", "lon", None), P("lat", "lon", None), P(), P(), P()),
        out_specs=(P("lat", "lon", None), P()),
        check_vma=False,
    )
```

```python
import functools
import math

import jax
import jax.numpy as jnp
from jax import lax
from jax.experimental import pallas as pl
from jax.experimental.pallas import tpu as pltpu
from jax.sharding import PartitionSpec as P

F32 = jnp.float32
BF16 = jnp.bfloat16
BOTH = ("lat", "lon")
WIDE = 48
WIN = 32


def coords(index):
    lat, lon = divmod(index, 16)
    return {"z": lat // 2, "x": lat % 2 * 2 + lon // 2 % 2, "y": lon // 4, "c": lon % 2}


def index_of(at):
    return (at["z"] * 2 + at["x"] // 2) * 16 + at["y"] * 4 + at["x"] % 2 * 2 + at["c"]


def route(**moves):
    pairs = []
    for source in range(256):
        at = coords(source)
        for axis, move in moves.items():
            at[axis] = move(at[axis])
        pairs.append((source, index_of(at)))
    return pairs


def flip(v):
    return v ^ 1


CORE = route(c=flip)
PLANES = [
    [i for i in range(256) if coords(i)["z"] == z and coords(i)["c"] == c]
    for z in range(8)
    for c in range(2)
]
QUAD = [route(z=lambda v, m=m: v ^ m) for m in (1, 2, 3)]
MIRROR = route(z=lambda v: 7 - v)


def chain(odd, periodic):
    pairs = [(i, ((i + odd) ^ 1) - odd) for i in range(16)]
    return [(i, j % 16) for i, j in pairs if periodic or 0 <= j < 16]


def send(value, pairs):
    return lax.ppermute(value, BOTH, pairs)


def trade(blocks):
    return lax.all_to_all(blocks, BOTH, 0, 0, axis_index_groups=PLANES, tiled=True)


def whole(n):
    return [pl.BlockSpec(memory_space=pltpu.VMEM)] * n


SMEM = pl.BlockSpec(memory_space=pltpu.SMEM)
ANY = pl.BlockSpec(memory_space=pl.ANY)
PARAMS = pltpu.CompilerParams(vmem_limit_bytes=16 * 1024 * 1024)


def groups(u):
    return max(0, 2 * u - 4) // 4, min(11, 2 * u + 5) // 4


def extend_kernel(at_ref, block_ref, even_ref, odd_ref, ext_ref, to_even_ref, to_odd_ref):
    first = at_ref[0] == 0
    even, odd = even_ref[...], odd_ref[...]
    ext_ref[...] = jnp.zeros_like(ext_ref)
    ext_ref[:, :8] = jnp.where(first, odd, even)
    ext_ref[:, 8:53] = block_ref[...]
    ext_ref[:, 53:61] = jnp.where(first, even, odd)
    top, bottom = ext_ref[:4], ext_ref[8:]
    upper = at_ref[1] == 0
    to_even_ref[...] = jnp.where(upper, bottom, top)
    to_odd_ref[...] = jnp.where(upper, top, bottom)


def band_kernel(psi_ref, feat_ref, band_ref, rim_ref, middle_ref, edge_ref, wide_ref):
    wide_ref[...] = jnp.zeros_like(wide_ref)
    wide_ref[:, :45, :] = feat_ref[...]
    middle_ref[...] = wide_ref[4:8].reshape(4 * WIDE, 256).T
    edge = jnp.concatenate([wide_ref[:4], wide_ref[8:]], axis=0)
    edge_ref[...] = edge.reshape(8 * WIDE, 256).T
    place = lax.broadcasted_iota(jnp.int32, (9, 128), 1) // WIN

    def taps(p, start):
        total = jnp.zeros((9, 128), F32)
        for s in range(4):
            tap = p - start - s + 8
            if 0 <= tap <= 8:
                total = jnp.where(place == s, psi_ref[start + s, tap], total)
        return total

    def spread(line):
        line = jnp.broadcast_to(line, (16, 128))
        return pltpu.roll(line, 0, 1, stride=1, stride_axis=0).astype(BF16)

    for u in range(6):
        low, high = groups(u)
        for pp in range(2):
            p = 2 * u + pp
            for g in range(low, high + 1):
                total = taps(p, 4 + 4 * g)
                for k in range(9):
                    first = (pp * 9 + k) * 16
                    band_ref[u, first : first + 16, 128 * g : 128 * g + 128] = spread(total[k : k + 1])
            if u in (0, 1, 4, 5):
                total = taps(p, 0 if u < 2 else 16)
                for k in range(9):
                    first = (pp * 9 + k) * 16
                    rim_ref[u if u < 2 else u - 2, first : first + 16, :] = spread(total[k : k + 1])


def halves_of(core, ref):
    own = pl.multiple_of(core * 128, 128)
    other = pl.multiple_of(128 - core * 128, 128)
    return jnp.concatenate([ref[pl.ds(own, 128), :], ref[pl.ds(other, 128), :]], axis=0)


def own_kernel(at_ref, ext_ref, band_ref, feat_ref, y_ref, sums_ref, part_ref):
    for u in range(6):
        low, high = groups(u)
        band = band_ref[u, :, 128 * low : 128 * high + 128]
        for t in range(3):
            window = ext_ref[4 * low : 4 * high + 4, 16 * t : 16 * t + WIN, :].reshape(-1, 256)
            rows = jnp.dot(band, window, preferred_element_type=F32)
            if u in (2, 3):
                rows = rows.astype(BF16)
            for pp in range(2):
                start = (2 * u + pp) % 4 * WIDE + 16 * t
                for k in range(9):
                    first = (pp * 9 + k) * 16
                    if u in (2, 3):
                        y_ref[k, start : start + 16, :] = rows[first : first + 16]
            if u not in (2, 3):
                sums_ref[u if u < 2 else u - 2, t] = rows
    feat = halves_of(at_ref[0], feat_ref)
    for k in range(9):
        part_ref[k] = jnp.dot(feat, y_ref[k], preferred_element_type=F32)


def edge_kernel(at_ref, even_ref, odd_ref, rim_ref, sums_ref, part_ref, feat_ref, y_ref, keep_ref, send_ref):
    upper = at_ref[1] == 0
    for half in range(2):
        block = jnp.where(upper, odd_ref[...], even_ref[...])
        if half:
            block = jnp.where(upper, even_ref[...], odd_ref[...])
        for v in (2 * half, 2 * half + 1):
            rim = rim_ref[v]
            for t in range(3):
                window = block[:, 16 * t : 16 * t + WIN, :].reshape(-1, 256)
                rows = sums_ref[v, t] + jnp.dot(rim, window, preferred_element_type=F32)
                rows = rows.astype(BF16)
                for pp in range(2):
                    start = (2 * v + pp) * WIDE + 16 * t
                    for k in range(9):
                        first = (pp * 9 + k) * 16
                        y_ref[k, start : start + 16, :] = rows[first : first + 16]
    feat = halves_of(at_ref[0], feat_ref)
    for k in range(9):
        part = part_ref[k] + jnp.dot(feat, y_ref[k], preferred_element_type=F32)
        keep_ref[k] = part[:128]
        send_ref[k] = part[128:].astype(BF16)


def input_kernel(middle_ref, edge_ref, w_ref, out_ref):
    def mixed(ref, rows):
        total = jnp.zeros((rows * WIDE, 256), F32)
        for k in range(9):
            total += lax.dot_general(
                ref[k], w_ref[k], (((1,), (1,)), ((), ())), preferred_element_type=F32
            )
        return total.reshape(rows, WIDE, 256)[:, :45].astype(BF16)

    out_ref[4:8] = mixed(middle_ref, 4)
    edge = mixed(edge_ref, 8)
    out_ref[:4] = edge[:4]
    out_ref[8:] = edge[4:]


def split_kernel(keep_ref, got_ref, out_ref):
    for j in range(16):
        rows, cols = slice(j // 2 * 16, j // 2 * 16 + 16), slice(j % 2 * 128, j % 2 * 128 + 128)
        part = keep_ref[:, rows, cols] + got_ref[:, rows, cols].astype(F32)
        out_ref[j] = part.astype(BF16)


def sum_kernel(got_ref, out_ref):
    total = got_ref[0].astype(F32)
    for j in range(1, 16):
        total = total + got_ref[j].astype(F32)
    out_ref[...] = total.astype(BF16)


def join_kernel(scale, other, at_ref, blocks_ref, *refs):
    out_ref, half_ref, sems = refs[-3:]
    start = pl.multiple_of((at_ref[0] ^ other) * 128, 128)
    copies = []
    for k in range(9):
        for j in range(16):
            rows, cols = slice(j // 2 * 16, j // 2 * 16 + 16), slice(j % 2 * 128, j % 2 * 128 + 128)
            half_ref[k, rows, cols] = blocks_ref[j, k].astype(F32) * scale
        copy = pltpu.make_async_copy(half_ref.at[k], out_ref.at[k, pl.ds(start, 128), :], sems.at[k])
        copy.start()
        copies.append(copy)
    for copy in copies:
        copy.wait()


def call(kernel, outs, specs, *args, out_spec=None, scratch=(), aliases=None, **cost):
    estimate = pl.CostEstimate(transcendentals=0, **cost) if cost else None
    out_spec = out_spec or pl.BlockSpec(memory_space=pltpu.VMEM)
    return pl.pallas_call(
        kernel,
        out_shape=outs,
        in_specs=specs,
        out_specs=jax.tree.map(lambda _: out_spec, outs),
        scratch_shapes=scratch,
        input_output_aliases=aliases or {},
        compiler_params=PARAMS,
        cost_estimate=estimate,
    )(*args)


def shape(dims, dtype):
    return jax.ShapeDtypeStruct(dims, dtype)


def band_taps(quad_weights, reach_table):
    first = lax.axis_index("lat") * 12 - 4
    start = jnp.clip(first, 0, 192 - 20)
    psi = lax.dynamic_slice_in_dim(quad_weights, start, 20, 1)
    reach = lax.dynamic_slice_in_dim(reach_table, start, 20, 0)
    taps = lax.broadcasted_iota(jnp.int32, (1, 1, 1, 17), 3)
    psi = jnp.where(jnp.abs(taps - 8) <= reach[None, :, :, None], psi, jnp.zeros_like(psi))
    psi = jnp.pad(psi, ((0, 0), (4, 4), (0, 0), (0, 0)))
    psi = lax.dynamic_slice_in_dim(psi, first - start + 4, 20, 1)
    psi = jnp.pad(psi[..., ::-1], ((0, 0), (0, 0), (0, 0), (0, WIN - 17))).astype(F32)
    return jnp.concatenate([psi.transpose(1, 2, 0, 3)] * 4, axis=3)


def local(features, cotangent, weights, quad_weights, reach_table):
    core, upper = lax.axis_index("lon") % 2, lax.axis_index("lat") % 2
    at = jnp.stack([core, upper])

    west, east = cotangent[:, :8], cotangent[:, 37:]
    even = lax.ppermute(jnp.where(core == 0, east, west), "lon", chain(0, True))
    odd = lax.ppermute(jnp.where(core == 0, west, east), "lon", chain(1, True))
    psi = band_taps(quad_weights, reach_table)
    even, odd, psi = lax.optimization_barrier((even, odd, psi))
    rim = shape((4, 64, 256), BF16)
    ext, even, odd = call(
        extend_kernel, (shape((12, 64, 256), BF16), rim, rim), [SMEM] + whole(3), at, cotangent, even, odd
    )
    even = lax.ppermute(even, "lat", chain(0, False))
    odd = lax.ppermute(odd, "lat", chain(1, False))
    band, rims, feat, feat_edge = call(
        band_kernel,
        (
            shape((6, 288, 12 * WIN), BF16), shape((4, 288, 4 * WIN), BF16),
            shape((256, 4 * WIDE), BF16), shape((256, 8 * WIDE), BF16),
        ),
        whole(2), psi, features, scratch=[pltpu.VMEM((12, WIDE, 256), BF16)],
    )
    y, sums, part = call(
        own_kernel,
        (shape((9, 4 * WIDE, 256), BF16), shape((4, 3, 288, 256), F32), shape((9, 256, 256), F32)),
        [SMEM] + whole(3), at, ext, band, feat, flops=10**6, bytes_accessed=10**6,
    )
    even, odd, part = lax.optimization_barrier((even, odd, part))
    halves, blocks = (9, 128, 256), (16, 9, 16, 128)
    y_edge, keep, out = call(
        edge_kernel,
        (shape((9, 8 * WIDE, 256), BF16), shape(halves, F32), shape(halves, BF16)),
        [SMEM] + whole(6), at, even, odd, rims, sums, part, feat_edge,
    )
    got = send(out, CORE)
    got = trade(call(split_kernel, shape(blocks, BF16), whole(2), keep, got))
    mine = call(sum_kernel, shape(blocks[1:], BF16), whole(1), got)
    mine, y, y_edge = lax.optimization_barrier((mine, y, y_edge))
    gots = [send(mine, r).astype(F32) for r in QUAD]
    total = (mine.astype(F32) + gots[0]) + (gots[1] + gots[2])
    grad_input = call(
        input_kernel, shape((12, 45, 256), BF16), whole(3), y, y_edge, weights,
        flops=2 * 10**9, bytes_accessed=4 * 10**6,
    )
    mine = total.astype(BF16)
    got = send(mine, MIRROR)
    total = mine.astype(F32) + got.astype(F32)
    total, grad_input = lax.optimization_barrier((total, grad_input))
    own = trade(jnp.broadcast_to(total.astype(BF16), blocks))
    got = send(own, CORE)
    scale = 1.0 / math.sqrt(192 * 720)
    scratch = [pltpu.VMEM(halves, F32), pltpu.SemaphoreType.DMA((9,))]
    full = shape((9, 256, 256), F32)
    grad_weight = call(
        functools.partial(join_kernel, scale, 0), full, [SMEM] + whole(1), at, own,
        out_spec=ANY, scratch=scratch, flops=10**6, bytes_accessed=2 * 10**6,
    )
    grad_weight = call(
        functools.partial(join_kernel, scale, 1), full, [SMEM] + whole(1) + [ANY], at, got, grad_weight,
        out_spec=ANY, scratch=scratch, aliases={2: 0}, flops=10**6, bytes_accessed=2 * 10**6,
    )
    return grad_input, grad_weight


def solution(mesh):
    return jax.shard_map(
        local,
        mesh=mesh,
        in_specs=(P("lat", "lon", None), P("lat", "lon", None), P(), P(), P()),
        out_specs=(P("lat", "lon", None), P()),
        check_vma=False,
    )
```

```python
import functools
import math

import jax
import jax.numpy as jnp
from jax import lax
from jax.experimental import pallas as pl
from jax.experimental.pallas import tpu as pltpu
from jax.sharding import PartitionSpec as P

F32 = jnp.float32
BF16 = jnp.bfloat16
BOTH = ("lat", "lon")
WIDE = 48
WIN = 32


def coords(index):
    lat, lon = divmod(index, 16)
    return {"z": lat // 2, "x": lat % 2 * 2 + lon // 2 % 2, "y": lon // 4, "c": lon % 2}


def index_of(at):
    return (at["z"] * 2 + at["x"] // 2) * 16 + at["y"] * 4 + at["x"] % 2 * 2 + at["c"]


def route(**moves):
    pairs = []
    for source in range(256):
        at = coords(source)
        for axis, move in moves.items():
            at[axis] = move(at[axis])
        pairs.append((source, index_of(at)))
    return pairs


def flip(v):
    return v ^ 1


CORE = route(c=flip)
PLANES = [
    [i for i in range(256) if coords(i)["z"] == z and coords(i)["c"] == c]
    for z in range(8)
    for c in range(2)
]
QUAD = [route(z=lambda v, m=m: v ^ m) for m in (1, 2, 3)]
MIRROR = route(z=lambda v: 7 - v)


def chain(odd, periodic):
    pairs = [(i, ((i + odd) ^ 1) - odd) for i in range(16)]
    return [(i, j % 16) for i, j in pairs if periodic or 0 <= j < 16]


def send(value, pairs):
    return lax.ppermute(value, BOTH, pairs)


def trade(blocks):
    return lax.all_to_all(blocks, BOTH, 0, 0, axis_index_groups=PLANES, tiled=True)


def whole(n):
    return [pl.BlockSpec(memory_space=pltpu.VMEM)] * n


SMEM = pl.BlockSpec(memory_space=pltpu.SMEM)
ANY = pl.BlockSpec(memory_space=pl.ANY)
PARAMS = pltpu.CompilerParams(vmem_limit_bytes=16 * 1024 * 1024)


def groups(u):
    return max(0, 2 * u - 4) // 4, min(11, 2 * u + 5) // 4


def extend_kernel(at_ref, block_ref, even_ref, odd_ref, ext_ref, to_odd_ref, to_even_ref):
    first = at_ref[0] == 0
    even, odd = even_ref[...], odd_ref[...]
    ext_ref[...] = jnp.zeros_like(ext_ref)
    ext_ref[:, :8] = jnp.where(first, odd, even)
    ext_ref[:, 8:53] = block_ref[...]
    ext_ref[:, 53:61] = jnp.where(first, even, odd)
    top, bottom = ext_ref[:4], ext_ref[8:]
    upper = at_ref[1] == 0
    to_even_ref[...] = jnp.where(upper, bottom, top)
    to_odd_ref[...] = jnp.where(upper, top, bottom)


def band_kernel(psi_ref, feat_ref, band_ref, rim_ref, middle_ref, edge_ref, wide_ref):
    wide_ref[...] = jnp.zeros_like(wide_ref)
    wide_ref[:, :45, :] = feat_ref[...]
    middle_ref[...] = wide_ref[4:8].reshape(4 * WIDE, 256).T
    edge_ref[0] = wide_ref[:4].reshape(4 * WIDE, 256).T
    edge_ref[1] = wide_ref[8:].reshape(4 * WIDE, 256).T
    place = lax.broadcasted_iota(jnp.int32, (9, 128), 1) // WIN

    def taps(p, start):
        total = jnp.zeros((9, 128), F32)
        for s in range(4):
            tap = p - start - s + 8
            if 0 <= tap <= 8:
                total = jnp.where(place == s, psi_ref[start + s, tap], total)
        return total

    def spread(line):
        line = jnp.broadcast_to(line, (16, 128))
        return pltpu.roll(line, 0, 1, stride=1, stride_axis=0).astype(BF16)

    for u in range(6):
        low, high = groups(u)
        for pp in range(2):
            p = 2 * u + pp
            for g in range(low, high + 1):
                total = taps(p, 4 + 4 * g)
                for k in range(9):
                    first = (pp * 9 + k) * 16
                    band_ref[u, first : first + 16, 128 * g : 128 * g + 128] = spread(total[k : k + 1])
            if u in (0, 1, 4, 5):
                total = taps(p, 0 if u < 2 else 16)
                for k in range(9):
                    first = (pp * 9 + k) * 16
                    rim_ref[u // 4, u % 4, first : first + 16, :] = spread(total[k : k + 1])


def halves_of(core, ref):
    own = pl.multiple_of(core * 128, 128)
    other = pl.multiple_of(128 - core * 128, 128)
    return jnp.concatenate([ref[pl.ds(own, 128), :], ref[pl.ds(other, 128), :]], axis=0)


def own_kernel(at_ref, ext_ref, band_ref, feat_ref, y_ref, sums_ref, part_ref):
    for u in range(6):
        low, high = groups(u)
        band = band_ref[u, :, 128 * low : 128 * high + 128]
        for t in range(3):
            window = ext_ref[4 * low : 4 * high + 4, 16 * t : 16 * t + WIN, :].reshape(-1, 256)
            rows = jnp.dot(band, window, preferred_element_type=F32)
            if u in (2, 3):
                rows = rows.astype(BF16)
            for pp in range(2):
                start = (2 * u + pp) % 4 * WIDE + 16 * t
                for k in range(9):
                    first = (pp * 9 + k) * 16
                    if u in (2, 3):
                        y_ref[k, start : start + 16, :] = rows[first : first + 16]
            if u not in (2, 3):
                sums_ref[u // 4, u % 4, t] = rows
    feat = halves_of(at_ref[0], feat_ref)
    for k in range(9):
        part_ref[k] = jnp.dot(feat, y_ref[k], preferred_element_type=F32)


def edge_kernel(odd, at_ref, got_ref, rim_ref, sums_ref, part_ref, feat_ref, y_ref, *out_refs):
    side = at_ref[1] if odd else 1 - at_ref[1]
    for v in range(2):
        rim = rim_ref[side, v]
        for t in range(3):
            window = got_ref[:, 16 * t : 16 * t + WIN, :].reshape(-1, 256)
            rows = sums_ref[side, v, t] + jnp.dot(rim, window, preferred_element_type=F32)
            rows = rows.astype(BF16)
            for pp in range(2):
                start = (2 * v + pp) * WIDE + 16 * t
                for k in range(9):
                    first = (pp * 9 + k) * 16
                    y_ref[k, start : start + 16, :] = rows[first : first + 16]
    feat = halves_of(at_ref[0], feat_ref.at[side])
    for k in range(9):
        part = part_ref[k] + jnp.dot(feat, y_ref[k], preferred_element_type=F32)
        if not odd:
            out_refs[0][k] = part
        else:
            out_refs[0][k] = part[:128]
            out_refs[1][k] = part[128:].astype(BF16)


def input_kernel(at_ref, middle_ref, odd_ref, even_ref, w_ref, out_ref):
    total = jnp.zeros((12 * WIDE, 256), F32)
    for k in range(9):
        y = jnp.concatenate([middle_ref[k], odd_ref[k], even_ref[k]], axis=0)
        total += lax.dot_general(
            y, w_ref[k], (((1,), (1,)), ((), ())), preferred_element_type=F32
        )
    total = total.reshape(12, WIDE, 256)[:, :45].astype(BF16)
    out_ref[4:8] = total[:4]
    out_ref[pl.ds(8 * at_ref[1], 4)] = total[4:8]
    out_ref[pl.ds(8 - 8 * at_ref[1], 4)] = total[8:]


def split_kernel(keep_ref, got_ref, out_ref):
    for j in range(16):
        rows, cols = slice(j // 2 * 16, j // 2 * 16 + 16), slice(j % 2 * 128, j % 2 * 128 + 128)
        part = keep_ref[:, rows, cols] + got_ref[:, rows, cols].astype(F32)
        out_ref[j] = part.astype(BF16)


def sum_kernel(got_ref, out_ref):
    total = got_ref[0].astype(F32)
    for j in range(1, 16):
        total = total + got_ref[j].astype(F32)
    out_ref[...] = total.astype(BF16)


def join_kernel(scale, other, at_ref, blocks_ref, *refs):
    out_ref, half_ref, sem = refs[-3:]
    start = pl.multiple_of((at_ref[0] ^ other) * 128, 128)
    for j in range(16):
        rows, cols = slice(j // 2 * 16, j // 2 * 16 + 16), slice(j % 2 * 128, j % 2 * 128 + 128)
        half_ref[:, rows, cols] = blocks_ref[j].astype(F32) * scale
    copy = pltpu.make_async_copy(half_ref, out_ref.at[:, pl.ds(start, 128), :], sem)
    copy.start()
    copy.wait()


def call(kernel, outs, specs, *args, out_spec=None, scratch=(), aliases=None, **cost):
    estimate = pl.CostEstimate(transcendentals=0, **cost) if cost else None
    out_spec = out_spec or pl.BlockSpec(memory_space=pltpu.VMEM)
    return pl.pallas_call(
        kernel,
        out_shape=outs,
        in_specs=specs,
        out_specs=jax.tree.map(lambda _: out_spec, outs),
        scratch_shapes=scratch,
        input_output_aliases=aliases or {},
        compiler_params=PARAMS,
        cost_estimate=estimate,
    )(*args)


def shape(dims, dtype):
    return jax.ShapeDtypeStruct(dims, dtype)


def masked_taps(quad_weights, reach_table):
    first = lax.axis_index("lat") * 12 - 4
    start = jnp.clip(first, 0, 192 - 20)
    psi = lax.dynamic_slice_in_dim(quad_weights, start, 20, 1)
    reach = lax.dynamic_slice_in_dim(reach_table, start, 20, 0)
    taps = lax.broadcasted_iota(jnp.int32, (1, 1, 1, 17), 3)
    psi = jnp.where(jnp.abs(taps - 8) <= reach[None, :, :, None], psi, jnp.zeros_like(psi))
    return psi, first - start + 4


def turned_taps(psi, start):
    psi = jnp.pad(psi, ((0, 0), (4, 4), (0, 0), (0, 0)))
    psi = lax.dynamic_slice_in_dim(psi, start, 20, 1)
    psi = jnp.pad(psi[..., ::-1], ((0, 0), (0, 0), (0, 0), (0, WIN - 17))).astype(F32)
    return jnp.concatenate([psi.transpose(1, 2, 0, 3)] * 4, axis=3)


def local(features, cotangent, weights, quad_weights, reach_table):
    core, upper = lax.axis_index("lon") % 2, lax.axis_index("lat") % 2
    at = jnp.stack([core, upper])

    west, east = cotangent[:, :8], cotangent[:, 37:]
    even = lax.ppermute(jnp.where(core == 0, east, west), "lon", chain(0, True))
    odd = lax.ppermute(jnp.where(core == 0, west, east), "lon", chain(1, True))
    psi, start = masked_taps(quad_weights, reach_table)
    even, odd, psi = lax.optimization_barrier((even, odd, psi))
    rim = shape((4, 64, 256), BF16)
    ext, odd, even = call(
        extend_kernel, (shape((12, 64, 256), BF16), rim, rim), [SMEM] + whole(3), at, cotangent, even, odd
    )
    odd = lax.ppermute(odd, "lat", chain(1, False))
    even = lax.ppermute(even, "lat", chain(0, False))
    side = (9, 4 * WIDE, 256)
    band, rims, feat, feat_edge = call(
        band_kernel,
        (
            shape((6, 288, 12 * WIN), BF16), shape((2, 2, 288, 4 * WIN), BF16),
            shape((256, 4 * WIDE), BF16), shape((2, 256, 4 * WIDE), BF16),
        ),
        whole(2), turned_taps(psi, start), features, scratch=[pltpu.VMEM((12, WIDE, 256), BF16)],
    )
    y, sums, part = call(
        own_kernel, (shape(side, BF16), shape((2, 2, 3, 288, 256), F32), shape((9, 256, 256), F32)),
        [SMEM] + whole(3), at, ext, band, feat, flops=10**6, bytes_accessed=10**6,
    )
    even, part = lax.optimization_barrier((even, part))
    y_even, part = call(
        functools.partial(edge_kernel, False), (shape(side, BF16), shape((9, 256, 256), F32)),
        [SMEM] + whole(5), at, even, rims, sums, part, feat_edge, flops=10**6, bytes_accessed=10**6,
    )
    odd, part = lax.optimization_barrier((odd, part))
    halves, blocks = (9, 128, 256), (16, 9, 16, 128)
    y_odd, keep, out = call(
        functools.partial(edge_kernel, True),
        (shape(side, BF16), shape(halves, F32), shape(halves, BF16)),
        [SMEM] + whole(5), at, odd, rims, sums, part, feat_edge,
    )
    got = send(out, CORE)
    got = trade(call(split_kernel, shape(blocks, BF16), whole(2), keep, got))
    mine = call(sum_kernel, shape(blocks[1:], BF16), whole(1), got)
    mine, y, y_odd, y_even = lax.optimization_barrier((mine, y, y_odd, y_even))
    gots = [send(mine, r).astype(F32) for r in QUAD]
    total = (mine.astype(F32) + gots[0]) + (gots[1] + gots[2])
    grad_input = call(
        input_kernel, shape((12, 45, 256), BF16), [SMEM] + whole(4), at, y, y_odd, y_even, weights,
        flops=2 * 10**9, bytes_accessed=4 * 10**6,
    )
    mine = total.astype(BF16)
    got = send(mine, MIRROR)
    total = mine.astype(F32) + got.astype(F32)
    total, grad_input = lax.optimization_barrier((total, grad_input))
    own = trade(jnp.broadcast_to(total.astype(BF16), blocks))
    got = send(own, CORE)
    scale = 1.0 / math.sqrt(192 * 720)
    scratch = [pltpu.VMEM(halves, F32), pltpu.SemaphoreType.DMA]
    full = shape((9, 256, 256), F32)
    grad_weight = call(
        functools.partial(join_kernel, scale, 0), full, [SMEM] + whole(1), at, own,
        out_spec=ANY, scratch=scratch, flops=10**6, bytes_accessed=2 * 10**6,
    )
    grad_weight = call(
        functools.partial(join_kernel, scale, 1), full, [SMEM] + whole(1) + [ANY], at, got, grad_weight,
        out_spec=ANY, scratch=scratch, aliases={2: 0}, flops=10**6, bytes_accessed=2 * 10**6,
    )
    return grad_input, grad_weight


def solution(mesh):
    return jax.shard_map(
        local,
        mesh=mesh,
        in_specs=(P("lat", "lon", None), P("lat", "lon", None), P(), P(), P()),
        out_specs=(P("lat", "lon", None), P()),
        check_vma=False,
    )
```

```python
import functools
import math

import jax
import jax.numpy as jnp
from jax import lax
from jax.experimental import pallas as pl
from jax.experimental.pallas import tpu as pltpu
from jax.sharding import PartitionSpec as P

F32 = jnp.float32
BF16 = jnp.bfloat16
BOTH = ("lat", "lon")
WIDE = 48
WIN = 32


def coords(index):
    lat, lon = divmod(index, 16)
    return {"z": lat // 2, "x": lat % 2 * 2 + lon // 2 % 2, "y": lon // 4, "c": lon % 2}


def index_of(at):
    return (at["z"] * 2 + at["x"] // 2) * 16 + at["y"] * 4 + at["x"] % 2 * 2 + at["c"]


def route(**moves):
    pairs = []
    for source in range(256):
        at = coords(source)
        for axis, move in moves.items():
            at[axis] = move(at[axis])
        pairs.append((source, index_of(at)))
    return pairs


def flip(v):
    return v ^ 1


CORE = route(c=flip)
PLANES = [
    [i for i in range(256) if coords(i)["z"] == z and coords(i)["c"] == c]
    for z in range(8)
    for c in range(2)
]
QUAD = [route(z=lambda v, m=m: v ^ m) for m in (1, 2, 3)]
MIRROR = route(z=lambda v: 7 - v)


def chain(odd, periodic):
    pairs = [(i, ((i + odd) ^ 1) - odd) for i in range(16)]
    return [(i, j % 16) for i, j in pairs if periodic or 0 <= j < 16]


def send(value, pairs):
    return lax.ppermute(value, BOTH, pairs)


def trade(blocks):
    return lax.all_to_all(blocks, BOTH, 0, 0, axis_index_groups=PLANES, tiled=True)


def whole(n):
    return [pl.BlockSpec(memory_space=pltpu.VMEM)] * n


ANY = pl.BlockSpec(memory_space=pl.ANY)
PARAMS = pltpu.CompilerParams(vmem_limit_bytes=16 * 1024 * 1024)


def groups(u):
    return max(0, 2 * u - 4) // 4, min(11, 2 * u + 5) // 4


def extend_kernel(block_ref, even_ref, odd_ref, ext_ref, to_even_ref, to_odd_ref):
    first = core_of() == 0
    even, odd = even_ref[...], odd_ref[...]
    ext_ref[...] = jnp.zeros_like(ext_ref)
    ext_ref[:, :8] = jnp.where(first, odd, even)
    ext_ref[:, 8:53] = block_ref[...]
    ext_ref[:, 53:61] = jnp.where(first, even, odd)
    top, bottom = ext_ref[:4], ext_ref[8:]
    upper = lax.axis_index("lat") % 2 == 0
    to_even_ref[...] = jnp.where(upper, bottom, top)
    to_odd_ref[...] = jnp.where(upper, top, bottom)


def band_kernel(psi_ref, feat_ref, band_ref, rim_ref, middle_ref, edge_ref, wide_ref):
    wide_ref[...] = jnp.zeros_like(wide_ref)
    wide_ref[:, :45, :] = feat_ref[...]
    middle_ref[...] = wide_ref[4:8].reshape(4 * WIDE, 256).T
    edge = jnp.concatenate([wide_ref[:4], wide_ref[8:]], axis=0)
    edge_ref[...] = edge.reshape(8 * WIDE, 256).T
    place = lax.broadcasted_iota(jnp.int32, (9, 128), 1) // WIN

    def taps(p, start):
        total = jnp.zeros((9, 128), F32)
        for s in range(4):
            tap = p - start - s + 8
            if 0 <= tap <= 8:
                total = jnp.where(place == s, psi_ref[start + s, tap], total)
        return total

    def spread(line):
        line = jnp.broadcast_to(line, (16, 128))
        return pltpu.roll(line, 0, 1, stride=1, stride_axis=0).astype(BF16)

    for u in range(6):
        low, high = groups(u)
        for pp in range(2):
            p = 2 * u + pp
            for g in range(low, high + 1):
                total = taps(p, 4 + 4 * g)
                for k in range(9):
                    first = (pp * 9 + k) * 16
                    band_ref[u, first : first + 16, 128 * g : 128 * g + 128] = spread(total[k : k + 1])
            if u in (0, 1, 4, 5):
                total = taps(p, 0 if u < 2 else 16)
                for k in range(9):
                    first = (pp * 9 + k) * 16
                    rim_ref[u if u < 2 else u - 2, first : first + 16, :] = spread(total[k : k + 1])


def core_of():
    return lax.axis_index("lon") % 2


def halves_of(ref):
    core = core_of()
    own = pl.multiple_of(core * 128, 128)
    other = pl.multiple_of(128 - core * 128, 128)
    return jnp.concatenate([ref[pl.ds(own, 128), :], ref[pl.ds(other, 128), :]], axis=0)


def own_kernel(ext_ref, band_ref, feat_ref, y_ref, sums_ref, part_ref):
    for u in range(6):
        low, high = groups(u)
        band = band_ref[u, :, 128 * low : 128 * high + 128]
        for t in range(3):
            window = ext_ref[4 * low : 4 * high + 4, 16 * t : 16 * t + WIN, :].reshape(-1, 256)
            rows = jnp.dot(band, window, preferred_element_type=F32)
            if u in (2, 3):
                rows = rows.astype(BF16)
            for pp in range(2):
                start = (2 * u + pp) % 4 * WIDE + 16 * t
                for k in range(9):
                    first = (pp * 9 + k) * 16
                    if u in (2, 3):
                        y_ref[k, start : start + 16, :] = rows[first : first + 16]
            if u not in (2, 3):
                sums_ref[u if u < 2 else u - 2, t] = rows
    feat = halves_of(feat_ref)
    for k in range(9):
        part_ref[k] = jnp.dot(feat, y_ref[k], preferred_element_type=F32)


def edge_kernel(even_ref, odd_ref, rim_ref, sums_ref, part_ref, feat_ref, y_ref, keep_ref, send_ref):
    upper = lax.axis_index("lat") % 2 == 0
    for half in range(2):
        block = jnp.where(upper, odd_ref[...], even_ref[...])
        if half:
            block = jnp.where(upper, even_ref[...], odd_ref[...])
        for v in (2 * half, 2 * half + 1):
            rim = rim_ref[v]
            for t in range(3):
                window = block[:, 16 * t : 16 * t + WIN, :].reshape(-1, 256)
                rows = sums_ref[v, t] + jnp.dot(rim, window, preferred_element_type=F32)
                rows = rows.astype(BF16)
                for pp in range(2):
                    start = (2 * v + pp) * WIDE + 16 * t
                    for k in range(9):
                        first = (pp * 9 + k) * 16
                        y_ref[k, start : start + 16, :] = rows[first : first + 16]
    feat = halves_of(feat_ref)
    for k in range(9):
        part = part_ref[k] + jnp.dot(feat, y_ref[k], preferred_element_type=F32)
        keep_ref[k] = part[:128]
        send_ref[k] = part[128:].astype(BF16)


def input_kernel(middle_ref, edge_ref, w_ref, out_ref):
    def mixed(ref, rows):
        total = jnp.zeros((rows * WIDE, 256), F32)
        for k in range(9):
            total += lax.dot_general(
                ref[k], w_ref[k], (((1,), (1,)), ((), ())), preferred_element_type=F32
            )
        return total.reshape(rows, WIDE, 256)[:, :45].astype(BF16)

    out_ref[4:8] = mixed(middle_ref, 4)
    edge = mixed(edge_ref, 8)
    out_ref[:4] = edge[:4]
    out_ref[8:] = edge[4:]


def split_kernel(keep_ref, got_ref, out_ref):
    for j in range(16):
        rows, cols = slice(j // 2 * 16, j // 2 * 16 + 16), slice(j % 2 * 128, j % 2 * 128 + 128)
        part = keep_ref[:, rows, cols] + got_ref[:, rows, cols].astype(F32)
        out_ref[j] = part.astype(BF16)


def sum_kernel(got_ref, out_ref):
    total = got_ref[0].astype(F32)
    for j in range(1, 16):
        total = total + got_ref[j].astype(F32)
    out_ref[...] = total.astype(BF16)


def join_kernel(scale, other, blocks_ref, *refs):
    out_ref, half_ref, sem = refs[-3:]
    start = pl.multiple_of((core_of() ^ other) * 128, 128)
    for j in range(16):
        rows, cols = slice(j // 2 * 16, j // 2 * 16 + 16), slice(j % 2 * 128, j % 2 * 128 + 128)
        half_ref[:, rows, cols] = blocks_ref[j].astype(F32) * scale
    copy = pltpu.make_async_copy(half_ref, out_ref.at[:, pl.ds(start, 128), :], sem)
    copy.start()
    copy.wait()


def call(kernel, outs, specs, *args, out_spec=None, scratch=(), aliases=None, **cost):
    estimate = pl.CostEstimate(transcendentals=0, **cost) if cost else None
    out_spec = out_spec or pl.BlockSpec(memory_space=pltpu.VMEM)
    return pl.pallas_call(
        kernel,
        out_shape=outs,
        in_specs=specs,
        out_specs=jax.tree.map(lambda _: out_spec, outs),
        scratch_shapes=scratch,
        input_output_aliases=aliases or {},
        compiler_params=PARAMS,
        cost_estimate=estimate,
    )(*args)


def shape(dims, dtype):
    return jax.ShapeDtypeStruct(dims, dtype)


def masked_taps(quad_weights, reach_table):
    first = lax.axis_index("lat") * 12 - 4
    start = jnp.clip(first, 0, 192 - 20)
    psi = lax.dynamic_slice_in_dim(quad_weights, start, 20, 1)
    reach = lax.dynamic_slice_in_dim(reach_table, start, 20, 0)
    taps = lax.broadcasted_iota(jnp.int32, (1, 1, 1, 17), 3)
    psi = jnp.where(jnp.abs(taps - 8) <= reach[None, :, :, None], psi, jnp.zeros_like(psi))
    return psi, first - start + 4


def turned_taps(psi, start):
    psi = jnp.pad(psi, ((0, 0), (4, 4), (0, 0), (0, 0)))
    psi = lax.dynamic_slice_in_dim(psi, start, 20, 1)
    psi = jnp.pad(psi[..., ::-1], ((0, 0), (0, 0), (0, 0), (0, WIN - 17))).astype(F32)
    return jnp.concatenate([psi.transpose(1, 2, 0, 3)] * 4, axis=3)


def local(features, cotangent, weights, quad_weights, reach_table):
    core = core_of()

    west, east = cotangent[:, :8], cotangent[:, 37:]
    even = lax.ppermute(jnp.where(core == 0, east, west), "lon", chain(0, True))
    odd = lax.ppermute(jnp.where(core == 0, west, east), "lon", chain(1, True))
    psi, start = masked_taps(quad_weights, reach_table)
    even, odd, psi = lax.optimization_barrier((even, odd, psi))
    rim = shape((4, 64, 256), BF16)
    ext, even, odd = call(
        extend_kernel, (shape((12, 64, 256), BF16), rim, rim), whole(3), cotangent, even, odd
    )
    even = lax.ppermute(even, "lat", chain(0, False))
    odd = lax.ppermute(odd, "lat", chain(1, False))
    band, rims, feat, feat_edge = call(
        band_kernel,
        (
            shape((6, 288, 12 * WIN), BF16), shape((4, 288, 4 * WIN), BF16),
            shape((256, 4 * WIDE), BF16), shape((256, 8 * WIDE), BF16),
        ),
        whole(2), turned_taps(psi, start), features, scratch=[pltpu.VMEM((12, WIDE, 256), BF16)],
    )
    y, sums, part = call(
        own_kernel,
        (shape((9, 4 * WIDE, 256), BF16), shape((4, 3, 288, 256), F32), shape((9, 256, 256), F32)),
        whole(3), ext, band, feat, flops=10**6, bytes_accessed=10**6,
    )
    even, odd, part = lax.optimization_barrier((even, odd, part))
    halves, blocks = (9, 128, 256), (16, 9, 16, 128)
    y_edge, keep, out = call(
        edge_kernel,
        (shape((9, 8 * WIDE, 256), BF16), shape(halves, F32), shape(halves, BF16)),
        whole(6), even, odd, rims, sums, part, feat_edge,
    )
    got = send(out, CORE)
    got = trade(call(split_kernel, shape(blocks, BF16), whole(2), keep, got))
    mine = call(sum_kernel, shape(blocks[1:], BF16), whole(1), got)
    mine, y, y_edge = lax.optimization_barrier((mine, y, y_edge))
    gots = [send(mine, r).astype(F32) for r in QUAD]
    total = (mine.astype(F32) + gots[0]) + (gots[1] + gots[2])
    grad_input = call(
        input_kernel, shape((12, 45, 256), BF16), whole(3), y, y_edge, weights,
        flops=2 * 10**9, bytes_accessed=4 * 10**6,
    )
    mine = total.astype(BF16)
    got = send(mine, MIRROR)
    total = mine.astype(F32) + got.astype(F32)
    total, grad_input = lax.optimization_barrier((total, grad_input))
    own = trade(jnp.broadcast_to(total.astype(BF16), blocks))
    got = send(own, CORE)
    scale = 1.0 / math.sqrt(192 * 720)
    scratch = [pltpu.VMEM(halves, F32), pltpu.SemaphoreType.DMA]
    full = shape((9, 256, 256), F32)
    grad_weight = call(
        functools.partial(join_kernel, scale, 0), full, whole(1), own,
        out_spec=ANY, scratch=scratch, flops=10**6, bytes_accessed=2 * 10**6,
    )
    grad_weight = call(
        functools.partial(join_kernel, scale, 1), full, whole(1) + [ANY], got, grad_weight,
        out_spec=ANY, scratch=scratch, aliases={1: 0}, flops=10**6, bytes_accessed=2 * 10**6,
    )
    return grad_input, grad_weight


def solution(mesh):
    return jax.shard_map(
        local,
        mesh=mesh,
        in_specs=(P("lat", "lon", None), P("lat", "lon", None), P(), P(), P()),
        out_specs=(P("lat", "lon", None), P()),
        check_vma=False,
    )
```

```python
import functools
import math

import jax
import jax.numpy as jnp
from jax import lax
from jax.experimental import pallas as pl
from jax.experimental.pallas import tpu as pltpu
from jax.sharding import PartitionSpec as P

F32 = jnp.float32
BF16 = jnp.bfloat16
BOTH = ("lat", "lon")
WIDE = 48
WIN = 32


def coords(index):
    lat, lon = divmod(index, 16)
    return {"z": lat // 2, "x": lat % 2 * 2 + lon // 2 % 2, "y": lon // 4, "c": lon % 2}


def index_of(at):
    return (at["z"] * 2 + at["x"] // 2) * 16 + at["y"] * 4 + at["x"] % 2 * 2 + at["c"]


def route(**moves):
    pairs = []
    for source in range(256):
        at = coords(source)
        for axis, move in moves.items():
            at[axis] = move(at[axis])
        pairs.append((source, index_of(at)))
    return pairs


def flip(v):
    return v ^ 1


CORE = route(c=flip)
PLANES = [
    [i for i in range(256) if coords(i)["z"] == z and coords(i)["c"] == c]
    for z in range(8)
    for c in range(2)
]
QUAD = [route(z=lambda v, m=m: v ^ m) for m in (1, 2, 3)]
MIRROR = route(z=lambda v: 7 - v)


def chain(odd, periodic):
    pairs = [(i, ((i + odd) ^ 1) - odd) for i in range(16)]
    return [(i, j % 16) for i, j in pairs if periodic or 0 <= j < 16]


def send(value, pairs):
    return lax.ppermute(value, BOTH, pairs)


def trade(blocks):
    return lax.all_to_all(blocks, BOTH, 0, 0, axis_index_groups=PLANES, tiled=True)


def whole(n):
    return [pl.BlockSpec(memory_space=pltpu.VMEM)] * n


ANY = pl.BlockSpec(memory_space=pl.ANY)
PARAMS = pltpu.CompilerParams(vmem_limit_bytes=16 * 1024 * 1024)


def groups(u):
    return max(0, 2 * u - 4) // 4, min(11, 2 * u + 5) // 4


def extend_kernel(block_ref, even_ref, odd_ref, ext_ref, to_even_ref, to_odd_ref):
    first = core_of() == 0
    even, odd = even_ref[...], odd_ref[...]
    ext_ref[...] = jnp.zeros_like(ext_ref)
    ext_ref[:, :8] = jnp.where(first, odd, even)
    ext_ref[:, 8:53] = block_ref[...]
    ext_ref[:, 53:61] = jnp.where(first, even, odd)
    top, bottom = ext_ref[:4], ext_ref[8:]
    upper = lax.axis_index("lat") % 2 == 0
    to_even_ref[...] = jnp.where(upper, bottom, top)
    to_odd_ref[...] = jnp.where(upper, top, bottom)


def band_kernel(psi_ref, feat_ref, band_ref, rim_ref, middle_ref, edge_ref, wide_ref):
    wide_ref[...] = jnp.zeros_like(wide_ref)
    wide_ref[:, :45, :] = feat_ref[...]
    middle_ref[...] = wide_ref[4:8].reshape(4 * WIDE, 256).T
    edge = jnp.concatenate([wide_ref[:4], wide_ref[8:]], axis=0)
    edge_ref[...] = edge.reshape(8 * WIDE, 256).T
    place = lax.broadcasted_iota(jnp.int32, (9, 128), 1) // WIN
    lat = lax.axis_index("lat")
    moved = jnp.where(lat == 0, 4, jnp.where(lat == 15, -4, 0))

    def taps(p, start):
        total = jnp.zeros((9, 128), F32)
        for s in range(4):
            tap = p - start - s + 8
            if 0 <= tap <= 8:
                row = jnp.clip(start + s - moved, 0, 19)
                total = jnp.where(place == s, psi_ref[row, tap], total)
        return total

    def spread(line):
        line = jnp.broadcast_to(line, (16, 128))
        return pltpu.roll(line, 0, 1, stride=1, stride_axis=0).astype(BF16)

    for u in range(6):
        low, high = groups(u)
        for pp in range(2):
            p = 2 * u + pp
            for g in range(low, high + 1):
                total = taps(p, 4 + 4 * g)
                for k in range(9):
                    first = (pp * 9 + k) * 16
                    band_ref[u, first : first + 16, 128 * g : 128 * g + 128] = spread(total[k : k + 1])
            if u in (0, 1, 4, 5):
                total = taps(p, 0 if u < 2 else 16)
                for k in range(9):
                    first = (pp * 9 + k) * 16
                    rim_ref[u if u < 2 else u - 2, first : first + 16, :] = spread(total[k : k + 1])


def core_of():
    return lax.axis_index("lon") % 2


def halves_of(ref):
    core = core_of()
    own = pl.multiple_of(core * 128, 128)
    other = pl.multiple_of(128 - core * 128, 128)
    return jnp.concatenate([ref[pl.ds(own, 128), :], ref[pl.ds(other, 128), :]], axis=0)


def own_kernel(ext_ref, band_ref, feat_ref, y_ref, sums_ref, part_ref):
    for u in range(6):
        low, high = groups(u)
        band = band_ref[u, :, 128 * low : 128 * high + 128]
        for t in range(3):
            window = ext_ref[4 * low : 4 * high + 4, 16 * t : 16 * t + WIN, :].reshape(-1, 256)
            rows = jnp.dot(band, window, preferred_element_type=F32)
            if u in (2, 3):
                rows = rows.astype(BF16)
            for pp in range(2):
                start = (2 * u + pp) % 4 * WIDE + 16 * t
                for k in range(9):
                    first = (pp * 9 + k) * 16
                    if u in (2, 3):
                        y_ref[k, start : start + 16, :] = rows[first : first + 16]
            if u not in (2, 3):
                sums_ref[u if u < 2 else u - 2, t] = rows
    feat = halves_of(feat_ref)
    for k in range(9):
        part_ref[k] = jnp.dot(feat, y_ref[k], preferred_element_type=F32)


def edge_kernel(even_ref, odd_ref, rim_ref, sums_ref, part_ref, feat_ref, y_ref, keep_ref, send_ref):
    upper = lax.axis_index("lat") % 2 == 0
    for half in range(2):
        block = jnp.where(upper, odd_ref[...], even_ref[...])
        if half:
            block = jnp.where(upper, even_ref[...], odd_ref[...])
        for v in (2 * half, 2 * half + 1):
            rim = rim_ref[v]
            for t in range(3):
                window = block[:, 16 * t : 16 * t + WIN, :].reshape(-1, 256)
                rows = sums_ref[v, t] + jnp.dot(rim, window, preferred_element_type=F32)
                rows = rows.astype(BF16)
                for pp in range(2):
                    start = (2 * v + pp) * WIDE + 16 * t
                    for k in range(9):
                        first = (pp * 9 + k) * 16
                        y_ref[k, start : start + 16, :] = rows[first : first + 16]
    feat = halves_of(feat_ref)
    for k in range(9):
        part = part_ref[k] + jnp.dot(feat, y_ref[k], preferred_element_type=F32)
        keep_ref[k] = part[:128]
        send_ref[k] = part[128:].astype(BF16)


def input_kernel(middle_ref, edge_ref, w_ref, out_ref):
    def mixed(ref, rows):
        total = jnp.zeros((rows * WIDE, 256), F32)
        for k in range(9):
            total += lax.dot_general(
                ref[k], w_ref[k], (((1,), (1,)), ((), ())), preferred_element_type=F32
            )
        return total.reshape(rows, WIDE, 256)[:, :45].astype(BF16)

    out_ref[4:8] = mixed(middle_ref, 4)
    edge = mixed(edge_ref, 8)
    out_ref[:4] = edge[:4]
    out_ref[8:] = edge[4:]


def split_kernel(keep_ref, got_ref, out_ref):
    for j in range(16):
        rows, cols = slice(j // 2 * 16, j // 2 * 16 + 16), slice(j % 2 * 128, j % 2 * 128 + 128)
        part = keep_ref[:, rows, cols] + got_ref[:, rows, cols].astype(F32)
        out_ref[j] = part.astype(BF16)


def sum_kernel(got_ref, out_ref):
    total = got_ref[0].astype(F32)
    for j in range(1, 16):
        total = total + got_ref[j].astype(F32)
    out_ref[...] = total.astype(BF16)


def join_kernel(scale, other, blocks_ref, *refs):
    out_ref, half_ref, sem = refs[-3:]
    start = pl.multiple_of((core_of() ^ other) * 128, 128)
    for j in range(16):
        rows, cols = slice(j // 2 * 16, j // 2 * 16 + 16), slice(j % 2 * 128, j % 2 * 128 + 128)
        half_ref[:, rows, cols] = blocks_ref[j].astype(F32) * scale
    copy = pltpu.make_async_copy(half_ref, out_ref.at[:, pl.ds(start, 128), :], sem)
    copy.start()
    copy.wait()


def call(kernel, outs, specs, *args, out_spec=None, scratch=(), aliases=None, **cost):
    estimate = pl.CostEstimate(transcendentals=0, **cost) if cost else None
    out_spec = out_spec or pl.BlockSpec(memory_space=pltpu.VMEM)
    return pl.pallas_call(
        kernel,
        out_shape=outs,
        in_specs=specs,
        out_specs=jax.tree.map(lambda _: out_spec, outs),
        scratch_shapes=scratch,
        input_output_aliases=aliases or {},
        compiler_params=PARAMS,
        cost_estimate=estimate,
    )(*args)


def shape(dims, dtype):
    return jax.ShapeDtypeStruct(dims, dtype)


def masked_taps(quad_weights, reach_table):
    start = jnp.clip(lax.axis_index("lat") * 12 - 4, 0, 192 - 20)
    psi = lax.dynamic_slice_in_dim(quad_weights, start, 20, 1)
    reach = lax.dynamic_slice_in_dim(reach_table, start, 20, 0)
    taps = lax.broadcasted_iota(jnp.int32, (1, 1, 1, 17), 3)
    return jnp.where(jnp.abs(taps - 8) <= reach[None, :, :, None], psi, jnp.zeros_like(psi))


def turned_taps(psi):
    psi = jnp.pad(psi[..., ::-1], ((0, 0), (0, 0), (0, 0), (0, WIN - 17))).astype(F32)
    return jnp.concatenate([psi.transpose(1, 2, 0, 3)] * 4, axis=3)


def local(features, cotangent, weights, quad_weights, reach_table):
    core = core_of()

    west, east = cotangent[:, :8], cotangent[:, 37:]
    even = lax.ppermute(jnp.where(core == 0, east, west), "lon", chain(0, True))
    odd = lax.ppermute(jnp.where(core == 0, west, east), "lon", chain(1, True))
    psi = masked_taps(quad_weights, reach_table)
    even, odd, psi = lax.optimization_barrier((even, odd, psi))
    rim = shape((4, 64, 256), BF16)
    ext, even, odd = call(
        extend_kernel, (shape((12, 64, 256), BF16), rim, rim), whole(3), cotangent, even, odd
    )
    even = lax.ppermute(even, "lat", chain(0, False))
    odd = lax.ppermute(odd, "lat", chain(1, False))
    band, rims, feat, feat_edge = call(
        band_kernel,
        (
            shape((6, 288, 12 * WIN), BF16), shape((4, 288, 4 * WIN), BF16),
            shape((256, 4 * WIDE), BF16), shape((256, 8 * WIDE), BF16),
        ),
        whole(2), turned_taps(psi), features, scratch=[pltpu.VMEM((12, WIDE, 256), BF16)],
    )
    y, sums, part = call(
        own_kernel,
        (shape((9, 4 * WIDE, 256), BF16), shape((4, 3, 288, 256), F32), shape((9, 256, 256), F32)),
        whole(3), ext, band, feat, flops=10**6, bytes_accessed=10**6,
    )
    even, odd, part = lax.optimization_barrier((even, odd, part))
    halves, blocks = (9, 128, 256), (16, 9, 16, 128)
    y_edge, keep, out = call(
        edge_kernel,
        (shape((9, 8 * WIDE, 256), BF16), shape(halves, F32), shape(halves, BF16)),
        whole(6), even, odd, rims, sums, part, feat_edge,
    )
    got = send(out, CORE)
    got = trade(call(split_kernel, shape(blocks, BF16), whole(2), keep, got))
    mine = call(sum_kernel, shape(blocks[1:], BF16), whole(1), got)
    mine, y, y_edge = lax.optimization_barrier((mine, y, y_edge))
    gots = [send(mine, r).astype(F32) for r in QUAD]
    total = (mine.astype(F32) + gots[0]) + (gots[1] + gots[2])
    grad_input = call(
        input_kernel, shape((12, 45, 256), BF16), whole(3), y, y_edge, weights,
        flops=2 * 10**9, bytes_accessed=4 * 10**6,
    )
    mine = total.astype(BF16)
    got = send(mine, MIRROR)
    total = mine.astype(F32) + got.astype(F32)
    total, grad_input = lax.optimization_barrier((total, grad_input))
    own = trade(jnp.broadcast_to(total.astype(BF16), blocks))
    got = send(own, CORE)
    scale = 1.0 / math.sqrt(192 * 720)
    scratch = [pltpu.VMEM(halves, F32), pltpu.SemaphoreType.DMA]
    full = shape((9, 256, 256), F32)
    grad_weight = call(
        functools.partial(join_kernel, scale, 0), full, whole(1), own,
        out_spec=ANY, scratch=scratch, flops=10**6, bytes_accessed=2 * 10**6,
    )
    grad_weight = call(
        functools.partial(join_kernel, scale, 1), full, whole(1) + [ANY], got, grad_weight,
        out_spec=ANY, scratch=scratch, aliases={1: 0}, flops=10**6, bytes_accessed=2 * 10**6,
    )
    return grad_input, grad_weight


def solution(mesh):
    return jax.shard_map(
        local,
        mesh=mesh,
        in_specs=(P("lat", "lon", None), P("lat", "lon", None), P(), P(), P()),
        out_specs=(P("lat", "lon", None), P()),
        check_vma=False,
    )
```

```python
import functools
import math

import jax
import jax.numpy as jnp
from jax import lax
from jax.experimental import pallas as pl
from jax.experimental.pallas import tpu as pltpu
from jax.sharding import PartitionSpec as P

F32 = jnp.float32
BF16 = jnp.bfloat16
BOTH = ("lat", "lon")
WIDE = 48
WIN = 32


def coords(index):
    lat, lon = divmod(index, 16)
    return {"z": lat // 2, "x": lat % 2 * 2 + lon // 2 % 2, "y": lon // 4, "c": lon % 2}


def index_of(at):
    return (at["z"] * 2 + at["x"] // 2) * 16 + at["y"] * 4 + at["x"] % 2 * 2 + at["c"]


def route(**moves):
    pairs = []
    for source in range(256):
        at = coords(source)
        for axis, move in moves.items():
            at[axis] = move(at[axis])
        pairs.append((source, index_of(at)))
    return pairs


def flip(v):
    return v ^ 1


CORE = route(c=flip)
SLABS = [
    [i for i in range(256) if coords(i)["z"] // 2 == pair and coords(i)["c"] == c]
    for pair in range(4)
    for c in range(2)
]
QUAD = [route(z=lambda v, m=m: v ^ m) for m in (2, 4, 6)]


def chain(odd, periodic):
    pairs = [(i, ((i + odd) ^ 1) - odd) for i in range(16)]
    return [(i, j % 16) for i, j in pairs if periodic or 0 <= j < 16]


def send(value, pairs):
    return lax.ppermute(value, BOTH, pairs)


def trade(blocks):
    return lax.all_to_all(blocks, BOTH, 0, 0, axis_index_groups=SLABS, tiled=True)


def whole(n):
    return [pl.BlockSpec(memory_space=pltpu.VMEM)] * n


ANY = pl.BlockSpec(memory_space=pl.ANY)
PARAMS = pltpu.CompilerParams(vmem_limit_bytes=16 * 1024 * 1024)


def groups(u):
    return max(0, 2 * u - 4) // 4, min(11, 2 * u + 5) // 4


def rim_kernel(block_ref, even_ref, odd_ref, ext_ref):
    first = core_of() == 0
    west, east = block_ref[:, :8], block_ref[:, 37:]
    even_ref[...] = jnp.where(first, east, west)
    odd_ref[...] = jnp.where(first, west, east)
    ext_ref[...] = jnp.zeros_like(ext_ref)
    ext_ref[:, 8:53] = block_ref[...]


def extend_kernel(block_ref, even_ref, odd_ref, ext_ref, to_even_ref, to_odd_ref):
    first = core_of() == 0
    even, odd = even_ref[...], odd_ref[...]
    ext_ref[...] = block_ref[...]
    ext_ref[:, :8] = jnp.where(first, odd, even)
    ext_ref[:, 53:61] = jnp.where(first, even, odd)
    top, bottom = ext_ref[:4], ext_ref[8:]
    upper = lax.axis_index("lat") % 2 == 0
    to_even_ref[...] = jnp.where(upper, bottom, top)
    to_odd_ref[...] = jnp.where(upper, top, bottom)


def band_kernel(quad_ref, reach_ref, feat_ref, band_ref, rim_ref, middle_ref, edge_ref, wide_ref, flat_ref, turn_ref):
    wide_ref[...] = jnp.zeros_like(wide_ref)
    wide_ref[:, :45, :] = feat_ref[...]
    middle_ref[...] = wide_ref[4:8].reshape(4 * WIDE, 256).T
    edge = jnp.concatenate([wide_ref[:4], wide_ref[8:]], axis=0)
    edge_ref[...] = edge.reshape(8 * WIDE, 256).T
    flat_ref[...] = jnp.zeros_like(flat_ref)
    taps = lax.broadcasted_iota(jnp.int32, (17, 192), 0)
    for a in range(9):
        keep = jnp.abs(taps - 8) <= reach_ref[a : a + 1, :]
        for k in range(9):
            first = (9 * k + a) * WIN
            line = jnp.where(keep, quad_ref[k, a].astype(F32), 0.0)
            flat_ref[first : first + 17, :] = line.astype(BF16)
    row = lax.axis_index("lat") * 12 - 4 + lax.broadcasted_iota(jnp.int32, (32, 192), 0)
    pick = (row == lax.broadcasted_iota(jnp.int32, (32, 192), 1)).astype(F32).astype(BF16)
    picked = lax.dot_general(
        pick, flat_ref[...], (((1,), (1,)), ((), ())), preferred_element_type=F32
    ).astype(BF16)
    r = lax.broadcasted_iota(jnp.int32, (128, 512), 0)
    c = lax.broadcasted_iota(jnp.int32, (128, 512), 1)
    turn = (r // WIN == c // 128) & (r % WIN + c % WIN == 16)
    turn = turn.astype(F32).astype(BF16)
    for m in range(21):
        part = jnp.dot(picked[:, 128 * m : 128 * m + 128], turn, preferred_element_type=F32)
        for i in range(4):
            turn_ref[4 * m + i] = part[:, 128 * i : 128 * i + 128]
    place = lax.broadcasted_iota(jnp.int32, (16, 128), 1) // WIN

    def spread(p, k, start):
        total = jnp.zeros((16, 128), F32)
        for s in range(4):
            tap = p - start - s + 8
            if 0 <= tap <= 8:
                line = turn_ref[9 * k + tap, start + s : start + s + 1, :]
                total = jnp.where(place == s, jnp.broadcast_to(line, (16, 128)), total)
        return pltpu.roll(total, 0, 1, stride=1, stride_axis=0).astype(BF16)

    for u in range(6):
        low, high = groups(u)
        for pp in range(2):
            p = 2 * u + pp
            for k in range(9):
                first = (pp * 9 + k) * 16
                for g in range(low, high + 1):
                    lanes = slice(128 * g, 128 * g + 128)
                    band_ref[u, first : first + 16, lanes] = spread(p, k, 4 + 4 * g)
                if u in (0, 1, 4, 5):
                    rim_ref[u if u < 2 else u - 2, first : first + 16, :] = spread(p, k, 0 if u < 2 else 16)


def core_of():
    return lax.axis_index("lon") % 2


def halves_of(ref):
    core = core_of()
    own = pl.multiple_of(core * 128, 128)
    other = pl.multiple_of(128 - core * 128, 128)
    return jnp.concatenate([ref[pl.ds(own, 128), :], ref[pl.ds(other, 128), :]], axis=0)


def own_kernel(ext_ref, band_ref, feat_ref, y_ref, sums_ref, part_ref):
    for u in range(6):
        low, high = groups(u)
        band = band_ref[u, :, 128 * low : 128 * high + 128]
        for t in range(3):
            window = ext_ref[4 * low : 4 * high + 4, 16 * t : 16 * t + WIN, :].reshape(-1, 256)
            rows = jnp.dot(band, window, preferred_element_type=F32)
            if u in (2, 3):
                rows = rows.astype(BF16)
            for pp in range(2):
                start = (2 * u + pp) % 4 * WIDE + 16 * t
                for k in range(9):
                    first = (pp * 9 + k) * 16
                    if u in (2, 3):
                        y_ref[k, start : start + 16, :] = rows[first : first + 16]
            if u not in (2, 3):
                sums_ref[u if u < 2 else u - 2, t] = rows
    feat = halves_of(feat_ref)
    for k in range(9):
        part_ref[k] = jnp.dot(feat, y_ref[k], preferred_element_type=F32)


def edge_kernel(even_ref, odd_ref, rim_ref, sums_ref, part_ref, feat_ref, y_ref, send_ref):
    upper = lax.axis_index("lat") % 2 == 0
    for half in range(2):
        block = jnp.where(upper, odd_ref[...], even_ref[...])
        if half:
            block = jnp.where(upper, even_ref[...], odd_ref[...])
        for v in (2 * half, 2 * half + 1):
            rim = rim_ref[v]
            for t in range(3):
                window = block[:, 16 * t : 16 * t + WIN, :].reshape(-1, 256)
                rows = sums_ref[v, t] + jnp.dot(rim, window, preferred_element_type=F32)
                rows = rows.astype(BF16)
                for pp in range(2):
                    start = (2 * v + pp) * WIDE + 16 * t
                    for k in range(9):
                        first = (pp * 9 + k) * 16
                        y_ref[k, start : start + 16, :] = rows[first : first + 16]
    other = feat_ref[pl.ds(pl.multiple_of(128 - core_of() * 128, 128), 128), :]
    for k in range(9):
        part = part_ref[k, 128:] + jnp.dot(other, y_ref[k], preferred_element_type=F32)
        send_ref[k] = part.astype(BF16)


def keep_kernel(y_ref, part_ref, feat_ref, keep_ref):
    own = feat_ref[pl.ds(pl.multiple_of(core_of() * 128, 128), 128), :]
    for k in range(9):
        keep_ref[k] = part_ref[k, :128] + jnp.dot(own, y_ref[k], preferred_element_type=F32)


def input_kernel(middle_ref, edge_ref, w_ref, out_ref):
    def mixed(ref, rows):
        total = jnp.zeros((rows * WIDE, 256), F32)
        for k in range(9):
            total += lax.dot_general(
                ref[k], w_ref[k], (((1,), (1,)), ((), ())), preferred_element_type=F32
            )
        return total.reshape(rows, WIDE, 256)[:, :45].astype(BF16)

    out_ref[4:8] = mixed(middle_ref, 4)
    edge = mixed(edge_ref, 8)
    out_ref[:4] = edge[:4]
    out_ref[8:] = edge[4:]


def split_kernel(keep_ref, got_ref, out_ref):
    for i in range(16):
        rows, cols = slice(i // 2 * 16, i // 2 * 16 + 16), slice(i % 2 * 128, i % 2 * 128 + 128)
        part = keep_ref[:, rows, cols] + got_ref[:, rows, cols].astype(F32)
        j = i // 2 * 4 + i % 2
        out_ref[j] = part[:, :8].astype(BF16)
        out_ref[j + 2] = part[:, 8:].astype(BF16)


def sum_kernel(got_ref, out_ref):
    total = got_ref[0].astype(F32)
    for j in range(1, 32):
        total = total + got_ref[j].astype(F32)
    out_ref[...] = total.astype(BF16)


def join_kernel(scale, other, blocks_ref, *refs):
    out_ref, half_ref, sem = refs[-3:]
    start = pl.multiple_of((core_of() ^ other) * 128, 128)
    for j in range(32):
        rows, cols = slice(j // 2 * 8, j // 2 * 8 + 8), slice(j % 2 * 128, j % 2 * 128 + 128)
        half_ref[:, rows, cols] = blocks_ref[j].astype(F32) * scale
    copy = pltpu.make_async_copy(half_ref, out_ref.at[:, pl.ds(start, 128), :], sem)
    copy.start()
    copy.wait()


def call(kernel, outs, specs, *args, out_spec=None, scratch=(), aliases=None, **cost):
    estimate = pl.CostEstimate(transcendentals=0, **cost) if cost else None
    out_spec = out_spec or pl.BlockSpec(memory_space=pltpu.VMEM)
    return pl.pallas_call(
        kernel,
        out_shape=outs,
        in_specs=specs,
        out_specs=jax.tree.map(lambda _: out_spec, outs),
        scratch_shapes=scratch,
        input_output_aliases=aliases or {},
        compiler_params=PARAMS,
        cost_estimate=estimate,
    )(*args)


def shape(dims, dtype):
    return jax.ShapeDtypeStruct(dims, dtype)


def local(features, cotangent, weights, quad_weights, reach_table):
    slab = shape((12, 8, 256), BF16)
    even, odd, ext = call(
        rim_kernel, (slab, slab, shape((12, 64, 256), BF16)), whole(1), cotangent,
        flops=2 * 10**10, bytes_accessed=10**6,
    )
    even = lax.ppermute(even, "lon", chain(0, True))
    odd = lax.ppermute(odd, "lon", chain(1, True))
    band, rims, feat, feat_edge = call(
        band_kernel,
        (
            shape((6, 288, 12 * WIN), BF16), shape((4, 288, 4 * WIN), BF16),
            shape((256, 4 * WIDE), BF16), shape((256, 8 * WIDE), BF16),
        ),
        whole(3), quad_weights.transpose(0, 2, 3, 1), reach_table.T, features,
        scratch=[
            pltpu.VMEM((12, WIDE, 256), BF16), pltpu.VMEM((84 * WIN, 192), BF16), pltpu.VMEM((84, 32, 128), F32),
        ],
    )
    even, odd, band = lax.optimization_barrier((even, odd, band))
    rim = shape((4, 64, 256), BF16)
    ext, even, odd = call(
        extend_kernel, (shape((12, 64, 256), BF16), rim, rim), whole(3), ext, even, odd
    )
    even = lax.ppermute(even, "lat", chain(0, False))
    odd = lax.ppermute(odd, "lat", chain(1, False))
    y, sums, part = call(
        own_kernel,
        (shape((9, 4 * WIDE, 256), BF16), shape((4, 3, 288, 256), F32), shape((9, 256, 256), F32)),
        whole(3), ext, band, feat, flops=10**6, bytes_accessed=10**6,
    )
    even, odd, part = lax.optimization_barrier((even, odd, part))
    halves, blocks = (9, 128, 256), (32, 9, 8, 128)
    y_edge, out = call(
        edge_kernel, (shape((9, 8 * WIDE, 256), BF16), shape(halves, BF16)), whole(6),
        even, odd, rims, sums, part, feat_edge,
    )
    got = send(out, CORE)
    keep = call(
        keep_kernel, shape(halves, F32), whole(3), y_edge, part, feat_edge,
        flops=10**9, bytes_accessed=4 * 10**6,
    )
    got = trade(call(split_kernel, shape(blocks, BF16), whole(2), keep, got))
    mine = call(sum_kernel, shape(blocks[1:], BF16), whole(1), got)
    mine, y, y_edge = lax.optimization_barrier((mine, y, y_edge))
    gots = [send(mine, r).astype(F32) for r in QUAD]
    total = (mine.astype(F32) + gots[0]) + (gots[1] + gots[2])
    grad_input = call(
        input_kernel, shape((12, 45, 256), BF16), whole(3), y, y_edge, weights,
        flops=2 * 10**9, bytes_accessed=4 * 10**6,
    )
    total, grad_input = lax.optimization_barrier((total, grad_input))
    own = trade(jnp.broadcast_to(total.astype(BF16), blocks))
    got = send(own, CORE)
    scale = 1.0 / math.sqrt(192 * 720)
    scratch = [pltpu.VMEM(halves, F32), pltpu.SemaphoreType.DMA]
    full = shape((9, 256, 256), F32)
    grad_weight = call(
        functools.partial(join_kernel, scale, 0), full, whole(1), own,
        out_spec=ANY, scratch=scratch, flops=10**6, bytes_accessed=2 * 10**6,
    )
    grad_weight = call(
        functools.partial(join_kernel, scale, 1), full, whole(1) + [ANY], got, grad_weight,
        out_spec=ANY, scratch=scratch, aliases={1: 0}, flops=10**6, bytes_accessed=2 * 10**6,
    )
    return grad_input, grad_weight


def solution(mesh):
    return jax.shard_map(
        local,
        mesh=mesh,
        in_specs=(P("lat", "lon", None), P("lat", "lon", None), P(), P(), P()),
        out_specs=(P("lat", "lon", None), P()),
        check_vma=False,
    )
```

```python
import functools
import math

import jax
import jax.numpy as jnp
from jax import lax
from jax.experimental import pallas as pl
from jax.experimental.pallas import tpu as pltpu
from jax.sharding import PartitionSpec as P

F32 = jnp.float32
BF16 = jnp.bfloat16
BOTH = ("lat", "lon")
WIDE = 48
WIN = 32


def coords(index):
    lat, lon = divmod(index, 16)
    return {"z": lat // 2, "x": lat % 2 * 2 + lon // 2 % 2, "y": lon // 4, "c": lon % 2}


def index_of(at):
    return (at["z"] * 2 + at["x"] // 2) * 16 + at["y"] * 4 + at["x"] % 2 * 2 + at["c"]


def route(**moves):
    pairs = []
    for source in range(256):
        at = coords(source)
        for axis, move in moves.items():
            at[axis] = move(at[axis])
        pairs.append((source, index_of(at)))
    return pairs


def flip(v):
    return v ^ 1


CORE = route(c=flip)
SLABS = [
    [i for i in range(256) if coords(i)["z"] // 2 == pair and coords(i)["c"] == c]
    for pair in range(4)
    for c in range(2)
]
QUAD = [route(z=lambda v, m=m: v ^ m) for m in (2, 6, 4)]


def chain(odd, periodic):
    pairs = [(i, ((i + odd) ^ 1) - odd) for i in range(16)]
    return [(i, j % 16) for i, j in pairs if periodic or 0 <= j < 16]


def send(value, pairs):
    return lax.ppermute(value, BOTH, pairs)


def trade(blocks):
    return lax.all_to_all(blocks, BOTH, 0, 0, axis_index_groups=SLABS, tiled=True)


def whole(n):
    return [pl.BlockSpec(memory_space=pltpu.VMEM)] * n


ANY = pl.BlockSpec(memory_space=pl.ANY)
PARAMS = pltpu.CompilerParams(vmem_limit_bytes=16 * 1024 * 1024)


def groups(u):
    return max(0, 2 * u - 4) // 4, min(11, 2 * u + 5) // 4


def rim_kernel(block_ref, even_ref, odd_ref, ext_ref):
    first = core_of() == 0
    west, east = block_ref[:, :8], block_ref[:, 37:]
    even_ref[...] = jnp.where(first, east, west)
    odd_ref[...] = jnp.where(first, west, east)
    ext_ref[...] = jnp.zeros_like(ext_ref)
    ext_ref[:, 8:53] = block_ref[...]


def extend_kernel(block_ref, even_ref, odd_ref, ext_ref, to_even_ref, to_odd_ref):
    first = core_of() == 0
    even, odd = even_ref[...], odd_ref[...]
    ext_ref[...] = block_ref[...]
    ext_ref[:, :8] = jnp.where(first, odd, even)
    ext_ref[:, 53:61] = jnp.where(first, even, odd)
    top, bottom = ext_ref[:4], ext_ref[8:]
    upper = lax.axis_index("lat") % 2 == 0
    to_even_ref[...] = jnp.where(upper, bottom, top)
    to_odd_ref[...] = jnp.where(upper, top, bottom)


def band_kernel(quad_ref, reach_ref, feat_ref, band_ref, rim_ref, middle_ref, edge_ref, wide_ref, flat_ref, turn_ref):
    wide_ref[...] = jnp.zeros_like(wide_ref)
    wide_ref[:, :45, :] = feat_ref[...]
    middle_ref[...] = wide_ref[4:8].reshape(4 * WIDE, 256).T
    edge = jnp.concatenate([wide_ref[:4], wide_ref[8:]], axis=0)
    edge_ref[...] = edge.reshape(8 * WIDE, 256).T
    flat_ref[...] = jnp.zeros_like(flat_ref)
    taps = lax.broadcasted_iota(jnp.int32, (17, 192), 0)
    for a in range(9):
        keep = jnp.abs(taps - 8) <= reach_ref[a : a + 1, :]
        for k in range(9):
            first = (9 * k + a) * WIN
            line = jnp.where(keep, quad_ref[k, a].astype(F32), 0.0)
            flat_ref[first : first + 17, :] = line.astype(BF16)
    row = lax.axis_index("lat") * 12 - 4 + lax.broadcasted_iota(jnp.int32, (32, 192), 0)
    pick = (row == lax.broadcasted_iota(jnp.int32, (32, 192), 1)).astype(F32).astype(BF16)
    picked = lax.dot_general(
        pick, flat_ref[...], (((1,), (1,)), ((), ())), preferred_element_type=F32
    ).astype(BF16)
    r = lax.broadcasted_iota(jnp.int32, (128, 512), 0)
    c = lax.broadcasted_iota(jnp.int32, (128, 512), 1)
    turn = (r // WIN == c // 128) & (r % WIN + c % WIN == 16)
    turn = turn.astype(F32).astype(BF16)
    for m in range(21):
        part = jnp.dot(picked[:, 128 * m : 128 * m + 128], turn, preferred_element_type=F32)
        for i in range(4):
            turn_ref[4 * m + i] = part[:, 128 * i : 128 * i + 128]
    place = lax.broadcasted_iota(jnp.int32, (16, 128), 1) // WIN

    def spread(p, k, start):
        total = jnp.zeros((16, 128), F32)
        for s in range(4):
            tap = p - start - s + 8
            if 0 <= tap <= 8:
                line = turn_ref[9 * k + tap, start + s : start + s + 1, :]
                total = jnp.where(place == s, jnp.broadcast_to(line, (16, 128)), total)
        return pltpu.roll(total, 0, 1, stride=1, stride_axis=0).astype(BF16)

    for u in range(6):
        low, high = groups(u)
        for pp in range(2):
            p = 2 * u + pp
            for k in range(9):
                first = (pp * 9 + k) * 16
                for g in range(low, high + 1):
                    lanes = slice(128 * g, 128 * g + 128)
                    band_ref[u, first : first + 16, lanes] = spread(p, k, 4 + 4 * g)
                if u in (0, 1, 4, 5):
                    rim_ref[u if u < 2 else u - 2, first : first + 16, :] = spread(p, k, 0 if u < 2 else 16)


def core_of():
    return lax.axis_index("lon") % 2


def halves_of(ref):
    core = core_of()
    own = pl.multiple_of(core * 128, 128)
    other = pl.multiple_of(128 - core * 128, 128)
    return jnp.concatenate([ref[pl.ds(own, 128), :], ref[pl.ds(other, 128), :]], axis=0)


def own_kernel(ext_ref, band_ref, feat_ref, y_ref, sums_ref, part_ref):
    for u in range(6):
        low, high = groups(u)
        band = band_ref[u, :, 128 * low : 128 * high + 128]
        for t in range(3):
            window = ext_ref[4 * low : 4 * high + 4, 16 * t : 16 * t + WIN, :].reshape(-1, 256)
            rows = jnp.dot(band, window, preferred_element_type=F32)
            if u in (2, 3):
                rows = rows.astype(BF16)
            for pp in range(2):
                start = (2 * u + pp) % 4 * WIDE + 16 * t
                for k in range(9):
                    first = (pp * 9 + k) * 16
                    if u in (2, 3):
                        y_ref[k, start : start + 16, :] = rows[first : first + 16]
            if u not in (2, 3):
                sums_ref[u if u < 2 else u - 2, t] = rows
    feat = halves_of(feat_ref)
    for k in range(9):
        part_ref[k] = jnp.dot(feat, y_ref[k], preferred_element_type=F32)


def edge_kernel(even_ref, odd_ref, rim_ref, sums_ref, part_ref, feat_ref, y_ref, send_ref):
    upper = lax.axis_index("lat") % 2 == 0
    for half in range(2):
        block = jnp.where(upper, odd_ref[...], even_ref[...])
        if half:
            block = jnp.where(upper, even_ref[...], odd_ref[...])
        for v in (2 * half, 2 * half + 1):
            rim = rim_ref[v]
            for t in range(3):
                window = block[:, 16 * t : 16 * t + WIN, :].reshape(-1, 256)
                rows = sums_ref[v, t] + jnp.dot(rim, window, preferred_element_type=F32)
                rows = rows.astype(BF16)
                for pp in range(2):
                    start = (2 * v + pp) * WIDE + 16 * t
                    for k in range(9):
                        first = (pp * 9 + k) * 16
                        y_ref[k, start : start + 16, :] = rows[first : first + 16]
    other = feat_ref[pl.ds(pl.multiple_of(128 - core_of() * 128, 128), 128), :]
    for k in range(9):
        part = part_ref[k, 128:] + jnp.dot(other, y_ref[k], preferred_element_type=F32)
        send_ref[k] = part.astype(BF16)


def keep_kernel(y_ref, part_ref, feat_ref, keep_ref):
    own = feat_ref[pl.ds(pl.multiple_of(core_of() * 128, 128), 128), :]
    for k in range(9):
        keep_ref[k] = part_ref[k, :128] + jnp.dot(own, y_ref[k], preferred_element_type=F32)


def input_kernel(middle_ref, edge_ref, w_ref, out_ref):
    def mixed(ref, rows):
        total = jnp.zeros((rows * WIDE, 256), F32)
        for k in range(9):
            total += lax.dot_general(
                ref[k], w_ref[k], (((1,), (1,)), ((), ())), preferred_element_type=F32
            )
        return total.reshape(rows, WIDE, 256)[:, :45].astype(BF16)

    out_ref[4:8] = mixed(middle_ref, 4)
    edge = mixed(edge_ref, 8)
    out_ref[:4] = edge[:4]
    out_ref[8:] = edge[4:]


def split_kernel(keep_ref, got_ref, out_ref):
    for i in range(16):
        rows, cols = slice(i // 2 * 16, i // 2 * 16 + 16), slice(i % 2 * 128, i % 2 * 128 + 128)
        part = keep_ref[:, rows, cols] + got_ref[:, rows, cols].astype(F32)
        j = i // 2 * 4 + i % 2
        out_ref[j] = part[:, :8].astype(BF16)
        out_ref[j + 2] = part[:, 8:].astype(BF16)


def sum_kernel(got_ref, out_ref):
    total = got_ref[0].astype(F32)
    for j in range(1, 32):
        total = total + got_ref[j].astype(F32)
    out_ref[...] = total.astype(BF16)


def join_kernel(scale, other, blocks_ref, *refs):
    out_ref, half_ref, sem = refs[-3:]
    start = pl.multiple_of((core_of() ^ other) * 128, 128)
    for j in range(32):
        rows, cols = slice(j // 2 * 8, j // 2 * 8 + 8), slice(j % 2 * 128, j % 2 * 128 + 128)
        half_ref[:, rows, cols] = blocks_ref[j].astype(F32) * scale
    copy = pltpu.make_async_copy(half_ref, out_ref.at[:, pl.ds(start, 128), :], sem)
    copy.start()
    copy.wait()


def call(kernel, outs, specs, *args, out_spec=None, scratch=(), aliases=None, **cost):
    estimate = pl.CostEstimate(transcendentals=0, **cost) if cost else None
    out_spec = out_spec or pl.BlockSpec(memory_space=pltpu.VMEM)
    return pl.pallas_call(
        kernel,
        out_shape=outs,
        in_specs=specs,
        out_specs=jax.tree.map(lambda _: out_spec, outs),
        scratch_shapes=scratch,
        input_output_aliases=aliases or {},
        compiler_params=PARAMS,
        cost_estimate=estimate,
    )(*args)


def shape(dims, dtype):
    return jax.ShapeDtypeStruct(dims, dtype)


def local(features, cotangent, weights, quad_weights, reach_table):
    slab = shape((12, 8, 256), BF16)
    even, odd, ext = call(
        rim_kernel, (slab, slab, shape((12, 64, 256), BF16)), whole(1), cotangent,
        flops=2 * 10**10, bytes_accessed=10**6,
    )
    even = lax.ppermute(even, "lon", chain(0, True))
    odd = lax.ppermute(odd, "lon", chain(1, True))
    band, rims, feat, feat_edge = call(
        band_kernel,
        (
            shape((6, 288, 12 * WIN), BF16), shape((4, 288, 4 * WIN), BF16),
            shape((256, 4 * WIDE), BF16), shape((256, 8 * WIDE), BF16),
        ),
        whole(3), quad_weights.transpose(0, 2, 3, 1), reach_table.T, features,
        scratch=[
            pltpu.VMEM((12, WIDE, 256), BF16), pltpu.VMEM((84 * WIN, 192), BF16), pltpu.VMEM((84, 32, 128), F32),
        ],
    )
    even, odd, band = lax.optimization_barrier((even, odd, band))
    rim = shape((4, 64, 256), BF16)
    ext, even, odd = call(
        extend_kernel, (shape((12, 64, 256), BF16), rim, rim), whole(3), ext, even, odd
    )
    even = lax.ppermute(even, "lat", chain(0, False))
    odd = lax.ppermute(odd, "lat", chain(1, False))
    y, sums, part = call(
        own_kernel,
        (shape((9, 4 * WIDE, 256), BF16), shape((4, 3, 288, 256), F32), shape((9, 256, 256), F32)),
        whole(3), ext, band, feat, flops=10**6, bytes_accessed=10**6,
    )
    even, odd, part = lax.optimization_barrier((even, odd, part))
    halves, blocks = (9, 128, 256), (32, 9, 8, 128)
    y_edge, out = call(
        edge_kernel, (shape((9, 8 * WIDE, 256), BF16), shape(halves, BF16)), whole(6),
        even, odd, rims, sums, part, feat_edge,
    )
    got = send(out, CORE)
    keep = call(
        keep_kernel, shape(halves, F32), whole(3), y_edge, part, feat_edge,
        flops=10**9, bytes_accessed=4 * 10**6,
    )
    got = trade(call(split_kernel, shape(blocks, BF16), whole(2), keep, got))
    mine = call(sum_kernel, shape(blocks[1:], BF16), whole(1), got)
    mine, y, y_edge = lax.optimization_barrier((mine, y, y_edge))
    gots = [send(mine, r).astype(F32) for r in QUAD]
    total = (mine.astype(F32) + gots[0]) + (gots[1] + gots[2])
    grad_input = call(
        input_kernel, shape((12, 45, 256), BF16), whole(3), y, y_edge, weights,
        flops=2 * 10**9, bytes_accessed=4 * 10**6,
    )
    total, grad_input = lax.optimization_barrier((total, grad_input))
    own = trade(jnp.broadcast_to(total.astype(BF16), blocks))
    got = send(own, CORE)
    scale = 1.0 / math.sqrt(192 * 720)
    scratch = [pltpu.VMEM(halves, F32), pltpu.SemaphoreType.DMA]
    full = shape((9, 256, 256), F32)
    grad_weight = call(
        functools.partial(join_kernel, scale, 0), full, whole(1), own,
        out_spec=ANY, scratch=scratch, flops=10**6, bytes_accessed=2 * 10**6,
    )
    grad_weight = call(
        functools.partial(join_kernel, scale, 1), full, whole(1) + [ANY], got, grad_weight,
        out_spec=ANY, scratch=scratch, aliases={1: 0}, flops=10**6, bytes_accessed=2 * 10**6,
    )
    return grad_input, grad_weight


def solution(mesh):
    return jax.shard_map(
        local,
        mesh=mesh,
        in_specs=(P("lat", "lon", None), P("lat", "lon", None), P(), P(), P()),
        out_specs=(P("lat", "lon", None), P()),
        check_vma=False,
    )
```

```python
import functools
import math

import jax
import jax.numpy as jnp
from jax import lax
from jax.experimental import pallas as pl
from jax.experimental.pallas import tpu as pltpu
from jax.sharding import PartitionSpec as P

F32 = jnp.float32
BF16 = jnp.bfloat16
BOTH = ("lat", "lon")
WIDE = 48
WIN = 32


def coords(index):
    lat, lon = divmod(index, 16)
    return {"z": lat // 2, "x": lat % 2 * 2 + lon // 2 % 2, "y": lon // 4, "c": lon % 2}


def index_of(at):
    return (at["z"] * 2 + at["x"] // 2) * 16 + at["y"] * 4 + at["x"] % 2 * 2 + at["c"]


def route(**moves):
    pairs = []
    for source in range(256):
        at = coords(source)
        for axis, move in moves.items():
            at[axis] = move(at[axis])
        pairs.append((source, index_of(at)))
    return pairs


def flip(v):
    return v ^ 1


CORE = route(c=flip)
SLABS = [
    [i for i in range(256) if coords(i)["z"] // 2 == pair and coords(i)["c"] == c]
    for pair in range(4)
    for c in range(2)
]
QUAD = [route(z=lambda v, m=m: v ^ m) for m in (2, 4, 6)]


def chain(odd, periodic):
    pairs = [(i, ((i + odd) ^ 1) - odd) for i in range(16)]
    return [(i, j % 16) for i, j in pairs if periodic or 0 <= j < 16]


def send(value, pairs):
    return lax.ppermute(value, BOTH, pairs)


def trade(blocks):
    return lax.all_to_all(blocks, BOTH, 0, 0, axis_index_groups=SLABS, tiled=True)


def whole(n):
    return [pl.BlockSpec(memory_space=pltpu.VMEM)] * n


ANY = pl.BlockSpec(memory_space=pl.ANY)
PARAMS = pltpu.CompilerParams(vmem_limit_bytes=16 * 1024 * 1024)


def groups(u):
    return max(0, 2 * u - 4) // 4, min(11, 2 * u + 5) // 4


def rim_kernel(block_ref, odd_ref, even_ref, ext_ref):
    first = core_of() == 0
    west, east = block_ref[:, :8], block_ref[:, 37:]
    even_ref[...] = jnp.where(first, east, west)
    odd_ref[...] = jnp.where(first, west, east)
    ext_ref[...] = jnp.zeros_like(ext_ref)
    ext_ref[:, 8:53] = block_ref[...]


def extend_kernel(block_ref, odd_ref, even_ref, ext_ref, to_even_ref, to_odd_ref):
    first = core_of() == 0
    even, odd = even_ref[...], odd_ref[...]
    ext_ref[...] = block_ref[...]
    ext_ref[:, :8] = jnp.where(first, odd, even)
    ext_ref[:, 53:61] = jnp.where(first, even, odd)
    top, bottom = ext_ref[:4], ext_ref[8:]
    upper = lax.axis_index("lat") % 2 == 0
    to_even_ref[...] = jnp.where(upper, bottom, top)
    to_odd_ref[...] = jnp.where(upper, top, bottom)


def band_kernel(quad_ref, reach_ref, feat_ref, band_ref, rim_ref, middle_ref, edge_ref, wide_ref, flat_ref, turn_ref):
    wide_ref[...] = jnp.zeros_like(wide_ref)
    wide_ref[:, :45, :] = feat_ref[...]
    middle_ref[...] = wide_ref[4:8].reshape(4 * WIDE, 256).T
    edge = jnp.concatenate([wide_ref[:4], wide_ref[8:]], axis=0)
    edge_ref[...] = edge.reshape(8 * WIDE, 256).T
    flat_ref[...] = jnp.zeros_like(flat_ref)
    taps = lax.broadcasted_iota(jnp.int32, (17, 192), 0)
    for a in range(9):
        keep = jnp.abs(taps - 8) <= reach_ref[a : a + 1, :]
        for k in range(9):
            first = (9 * k + a) * WIN
            line = jnp.where(keep, quad_ref[k, a].astype(F32), 0.0)
            flat_ref[first : first + 17, :] = line.astype(BF16)
    row = lax.axis_index("lat") * 12 - 4 + lax.broadcasted_iota(jnp.int32, (32, 192), 0)
    pick = (row == lax.broadcasted_iota(jnp.int32, (32, 192), 1)).astype(F32).astype(BF16)
    picked = lax.dot_general(
        pick, flat_ref[...], (((1,), (1,)), ((), ())), preferred_element_type=F32
    ).astype(BF16)
    r = lax.broadcasted_iota(jnp.int32, (128, 512), 0)
    c = lax.broadcasted_iota(jnp.int32, (128, 512), 1)
    turn = (r // WIN == c // 128) & (r % WIN + c % WIN == 16)
    turn = turn.astype(F32).astype(BF16)
    for m in range(21):
        part = jnp.dot(picked[:, 128 * m : 128 * m + 128], turn, preferred_element_type=F32)
        for i in range(4):
            turn_ref[4 * m + i] = part[:, 128 * i : 128 * i + 128]
    place = lax.broadcasted_iota(jnp.int32, (16, 128), 1) // WIN

    def spread(p, k, start):
        total = jnp.zeros((16, 128), F32)
        for s in range(4):
            tap = p - start - s + 8
            if 0 <= tap <= 8:
                line = turn_ref[9 * k + tap, start + s : start + s + 1, :]
                total = jnp.where(place == s, jnp.broadcast_to(line, (16, 128)), total)
        return pltpu.roll(total, 0, 1, stride=1, stride_axis=0).astype(BF16)

    for u in range(6):
        low, high = groups(u)
        for pp in range(2):
            p = 2 * u + pp
            for k in range(9):
                first = (pp * 9 + k) * 16
                for g in range(low, high + 1):
                    lanes = slice(128 * g, 128 * g + 128)
                    band_ref[u, first : first + 16, lanes] = spread(p, k, 4 + 4 * g)
                if u in (0, 1, 4, 5):
                    rim_ref[u if u < 2 else u - 2, first : first + 16, :] = spread(p, k, 0 if u < 2 else 16)


def core_of():
    return lax.axis_index("lon") % 2


def halves_of(ref):
    core = core_of()
    own = pl.multiple_of(core * 128, 128)
    other = pl.multiple_of(128 - core * 128, 128)
    return jnp.concatenate([ref[pl.ds(own, 128), :], ref[pl.ds(other, 128), :]], axis=0)


def own_kernel(ext_ref, band_ref, feat_ref, y_ref, sums_ref, part_ref):
    for u in range(6):
        low, high = groups(u)
        band = band_ref[u, :, 128 * low : 128 * high + 128]
        for t in range(3):
            window = ext_ref[4 * low : 4 * high + 4, 16 * t : 16 * t + WIN, :].reshape(-1, 256)
            rows = jnp.dot(band, window, preferred_element_type=F32)
            if u in (2, 3):
                rows = rows.astype(BF16)
            for pp in range(2):
                start = (2 * u + pp) % 4 * WIDE + 16 * t
                for k in range(9):
                    first = (pp * 9 + k) * 16
                    if u in (2, 3):
                        y_ref[k, start : start + 16, :] = rows[first : first + 16]
            if u not in (2, 3):
                sums_ref[u if u < 2 else u - 2, t] = rows
    feat = halves_of(feat_ref)
    for k in range(9):
        part_ref[k] = jnp.dot(feat, y_ref[k], preferred_element_type=F32)


def edge_kernel(even_ref, odd_ref, rim_ref, sums_ref, part_ref, feat_ref, y_ref, send_ref):
    upper = lax.axis_index("lat") % 2 == 0
    for half in range(2):
        block = jnp.where(upper, odd_ref[...], even_ref[...])
        if half:
            block = jnp.where(upper, even_ref[...], odd_ref[...])
        for v in (2 * half, 2 * half + 1):
            rim = rim_ref[v]
            for t in range(3):
                window = block[:, 16 * t : 16 * t + WIN, :].reshape(-1, 256)
                rows = sums_ref[v, t] + jnp.dot(rim, window, preferred_element_type=F32)
                rows = rows.astype(BF16)
                for pp in range(2):
                    start = (2 * v + pp) * WIDE + 16 * t
                    for k in range(9):
                        first = (pp * 9 + k) * 16
                        y_ref[k, start : start + 16, :] = rows[first : first + 16]
    other = feat_ref[pl.ds(pl.multiple_of(128 - core_of() * 128, 128), 128), :]
    for k in range(9):
        part = part_ref[k, 128:] + jnp.dot(other, y_ref[k], preferred_element_type=F32)
        send_ref[k] = part.astype(BF16)


def keep_kernel(y_ref, part_ref, feat_ref, keep_ref):
    own = feat_ref[pl.ds(pl.multiple_of(core_of() * 128, 128), 128), :]
    for k in range(9):
        keep_ref[k] = part_ref[k, :128] + jnp.dot(own, y_ref[k], preferred_element_type=F32)


def input_kernel(middle_ref, edge_ref, w_ref, out_ref):
    def mixed(ref, rows):
        total = jnp.zeros((rows * WIDE, 256), F32)
        for k in range(9):
            total += lax.dot_general(
                ref[k], w_ref[k], (((1,), (1,)), ((), ())), preferred_element_type=F32
            )
        return total.reshape(rows, WIDE, 256)[:, :45].astype(BF16)

    out_ref[4:8] = mixed(middle_ref, 4)
    edge = mixed(edge_ref, 8)
    out_ref[:4] = edge[:4]
    out_ref[8:] = edge[4:]


def split_kernel(keep_ref, got_ref, out_ref):
    for i in range(16):
        rows, cols = slice(i // 2 * 16, i // 2 * 16 + 16), slice(i % 2 * 128, i % 2 * 128 + 128)
        part = keep_ref[:, rows, cols] + got_ref[:, rows, cols].astype(F32)
        j = i // 2 * 4 + i % 2
        out_ref[j] = part[:, :8].astype(BF16)
        out_ref[j + 2] = part[:, 8:].astype(BF16)


def sum_kernel(got_ref, out_ref):
    total = got_ref[0].astype(F32)
    for j in range(1, 32):
        total = total + got_ref[j].astype(F32)
    out_ref[...] = total.astype(BF16)


def join_kernel(scale, other, blocks_ref, *refs):
    out_ref, half_ref, sem = refs[-3:]
    start = pl.multiple_of((core_of() ^ other) * 128, 128)
    for j in range(32):
        rows, cols = slice(j // 2 * 8, j // 2 * 8 + 8), slice(j % 2 * 128, j % 2 * 128 + 128)
        half_ref[:, rows, cols] = blocks_ref[j].astype(F32) * scale
    copy = pltpu.make_async_copy(half_ref, out_ref.at[:, pl.ds(start, 128), :], sem)
    copy.start()
    copy.wait()


def call(kernel, outs, specs, *args, out_spec=None, scratch=(), aliases=None, **cost):
    estimate = pl.CostEstimate(transcendentals=0, **cost) if cost else None
    out_spec = out_spec or pl.BlockSpec(memory_space=pltpu.VMEM)
    return pl.pallas_call(
        kernel,
        out_shape=outs,
        in_specs=specs,
        out_specs=jax.tree.map(lambda _: out_spec, outs),
        scratch_shapes=scratch,
        input_output_aliases=aliases or {},
        compiler_params=PARAMS,
        cost_estimate=estimate,
    )(*args)


def shape(dims, dtype):
    return jax.ShapeDtypeStruct(dims, dtype)


def local(features, cotangent, weights, quad_weights, reach_table):
    slab = shape((12, 8, 256), BF16)
    odd, even, ext = call(
        rim_kernel, (slab, slab, shape((12, 64, 256), BF16)), whole(1), cotangent,
        flops=2 * 10**10, bytes_accessed=10**6,
    )
    odd = lax.ppermute(odd, "lon", chain(1, True))
    even = lax.ppermute(even, "lon", chain(0, True))
    band, rims, feat, feat_edge = call(
        band_kernel,
        (
            shape((6, 288, 12 * WIN), BF16), shape((4, 288, 4 * WIN), BF16),
            shape((256, 4 * WIDE), BF16), shape((256, 8 * WIDE), BF16),
        ),
        whole(3), quad_weights.transpose(0, 2, 3, 1), reach_table.T, features,
        scratch=[
            pltpu.VMEM((12, WIDE, 256), BF16), pltpu.VMEM((84 * WIN, 192), BF16), pltpu.VMEM((84, 32, 128), F32),
        ],
    )
    odd, even, band = lax.optimization_barrier((odd, even, band))
    rim = shape((4, 64, 256), BF16)
    ext, even, odd = call(
        extend_kernel, (shape((12, 64, 256), BF16), rim, rim), whole(3), ext, odd, even
    )
    even = lax.ppermute(even, "lat", chain(0, False))
    odd = lax.ppermute(odd, "lat", chain(1, False))
    y, sums, part = call(
        own_kernel,
        (shape((9, 4 * WIDE, 256), BF16), shape((4, 3, 288, 256), F32), shape((9, 256, 256), F32)),
        whole(3), ext, band, feat, flops=10**6, bytes_accessed=10**6,
    )
    even, odd, part = lax.optimization_barrier((even, odd, part))
    halves, blocks = (9, 128, 256), (32, 9, 8, 128)
    y_edge, out = call(
        edge_kernel, (shape((9, 8 * WIDE, 256), BF16), shape(halves, BF16)), whole(6),
        even, odd, rims, sums, part, feat_edge,
    )
    got = send(out, CORE)
    keep = call(
        keep_kernel, shape(halves, F32), whole(3), y_edge, part, feat_edge,
        flops=10**9, bytes_accessed=4 * 10**6,
    )
    got = trade(call(split_kernel, shape(blocks, BF16), whole(2), keep, got))
    mine = call(sum_kernel, shape(blocks[1:], BF16), whole(1), got)
    mine, y, y_edge = lax.optimization_barrier((mine, y, y_edge))
    gots = [send(mine, r).astype(F32) for r in QUAD]
    total = (mine.astype(F32) + gots[0]) + (gots[1] + gots[2])
    grad_input = call(
        input_kernel, shape((12, 45, 256), BF16), whole(3), y, y_edge, weights,
        flops=2 * 10**9, bytes_accessed=4 * 10**6,
    )
    total, grad_input = lax.optimization_barrier((total, grad_input))
    own = trade(jnp.broadcast_to(total.astype(BF16), blocks))
    got = send(own, CORE)
    scale = 1.0 / math.sqrt(192 * 720)
    scratch = [pltpu.VMEM(halves, F32), pltpu.SemaphoreType.DMA]
    full = shape((9, 256, 256), F32)
    grad_weight = call(
        functools.partial(join_kernel, scale, 0), full, whole(1), own,
        out_spec=ANY, scratch=scratch, flops=10**6, bytes_accessed=2 * 10**6,
    )
    grad_weight = call(
        functools.partial(join_kernel, scale, 1), full, whole(1) + [ANY], got, grad_weight,
        out_spec=ANY, scratch=scratch, aliases={1: 0}, flops=10**6, bytes_accessed=2 * 10**6,
    )
    return grad_input, grad_weight


def solution(mesh):
    return jax.shard_map(
        local,
        mesh=mesh,
        in_specs=(P("lat", "lon", None), P("lat", "lon", None), P(), P(), P()),
        out_specs=(P("lat", "lon", None), P()),
        check_vma=False,
    )
```

```python
import functools
import math

import jax
import jax.numpy as jnp
from jax import lax
from jax.experimental import pallas as pl
from jax.experimental.pallas import tpu as pltpu
from jax.sharding import PartitionSpec as P

F32 = jnp.float32
BF16 = jnp.bfloat16
BOTH = ("lat", "lon")
WIDE = 48
WIN = 32


def coords(index):
    lat, lon = divmod(index, 16)
    return {"z": lat // 2, "x": lat % 2 * 2 + lon // 2 % 2, "y": lon // 4, "c": lon % 2}


def index_of(at):
    return (at["z"] * 2 + at["x"] // 2) * 16 + at["y"] * 4 + at["x"] % 2 * 2 + at["c"]


def route(**moves):
    pairs = []
    for source in range(256):
        at = coords(source)
        for axis, move in moves.items():
            at[axis] = move(at[axis])
        pairs.append((source, index_of(at)))
    return pairs


def flip(v):
    return v ^ 1


CORE = route(c=flip)
SLABS = [
    [i for i in range(256) if coords(i)["z"] // 2 == pair and coords(i)["c"] == c]
    for pair in range(4)
    for c in range(2)
]
QUAD = [route(z=lambda v, m=m: v ^ m) for m in (2, 4, 6)]


def chain(odd, periodic):
    pairs = [(i, ((i + odd) ^ 1) - odd) for i in range(16)]
    return [(i, j % 16) for i, j in pairs if periodic or 0 <= j < 16]


def send(value, pairs):
    return lax.ppermute(value, BOTH, pairs)


def trade(blocks):
    return lax.all_to_all(blocks, BOTH, 0, 0, axis_index_groups=SLABS, tiled=True)


def whole(n):
    return [pl.BlockSpec(memory_space=pltpu.VMEM)] * n


ANY = pl.BlockSpec(memory_space=pl.ANY)
PARAMS = pltpu.CompilerParams(vmem_limit_bytes=16 * 1024 * 1024)


def groups(u):
    return max(0, 2 * u - 4) // 4, min(11, 2 * u + 5) // 4


def rim_kernel(block_ref, even_ref, odd_ref, ext_ref):
    first = core_of() == 0
    west, east = block_ref[:, :8], block_ref[:, 37:]
    even_ref[...] = jnp.where(first, east, west)
    odd_ref[...] = jnp.where(first, west, east)
    ext_ref[...] = jnp.zeros_like(ext_ref)
    ext_ref[:, 8:53] = block_ref[...]


def extend_kernel(block_ref, even_ref, odd_ref, ext_ref, to_even_ref, to_odd_ref):
    first = core_of() == 0
    even, odd = even_ref[...], odd_ref[...]
    ext_ref[...] = block_ref[...]
    ext_ref[:, :8] = jnp.where(first, odd, even)
    ext_ref[:, 53:61] = jnp.where(first, even, odd)
    top, bottom = ext_ref[:4], ext_ref[8:]
    upper = lax.axis_index("lat") % 2 == 0
    to_even_ref[...] = jnp.where(upper, bottom, top)
    to_odd_ref[...] = jnp.where(upper, top, bottom)


def band_kernel(quad_ref, reach_ref, feat_ref, band_ref, rim_ref, middle_ref, edge_ref, wide_ref, flat_ref, turn_ref):
    wide_ref[...] = jnp.zeros_like(wide_ref)
    wide_ref[:, :45, :] = feat_ref[...]
    middle_ref[...] = wide_ref[4:8].reshape(4 * WIDE, 256).T
    edge = jnp.concatenate([wide_ref[:4], wide_ref[8:]], axis=0)
    edge_ref[...] = edge.reshape(8 * WIDE, 256).T
    flat_ref[...] = jnp.zeros_like(flat_ref)
    taps = lax.broadcasted_iota(jnp.int32, (17, 192), 0)
    for a in range(9):
        keep = jnp.abs(taps - 8) <= reach_ref[a : a + 1, :]
        for k in range(9):
            first = (9 * k + a) * WIN
            line = jnp.where(keep, quad_ref[k, a].astype(F32), 0.0)
            flat_ref[first : first + 17, :] = line.astype(BF16)
    row = lax.axis_index("lat") * 12 - 4 + lax.broadcasted_iota(jnp.int32, (32, 192), 0)
    pick = (row == lax.broadcasted_iota(jnp.int32, (32, 192), 1)).astype(F32).astype(BF16)
    picked = lax.dot_general(
        pick, flat_ref[...], (((1,), (1,)), ((), ())), preferred_element_type=F32
    ).astype(BF16)
    r = lax.broadcasted_iota(jnp.int32, (128, 512), 0)
    c = lax.broadcasted_iota(jnp.int32, (128, 512), 1)
    turn = (r // WIN == c // 128) & (r % WIN + c % WIN == 16)
    turn = turn.astype(F32).astype(BF16)
    for m in range(21):
        part = jnp.dot(picked[:, 128 * m : 128 * m + 128], turn, preferred_element_type=F32)
        for i in range(4):
            turn_ref[4 * m + i] = part[:, 128 * i : 128 * i + 128]
    place = lax.broadcasted_iota(jnp.int32, (16, 128), 1) // WIN

    def spread(p, k, start):
        total = jnp.zeros((16, 128), F32)
        for s in range(4):
            tap = p - start - s + 8
            if 0 <= tap <= 8:
                line = turn_ref[9 * k + tap, start + s : start + s + 1, :]
                total = jnp.where(place == s, jnp.broadcast_to(line, (16, 128)), total)
        return pltpu.roll(total, 0, 1, stride=1, stride_axis=0).astype(BF16)

    for u in range(6):
        low, high = groups(u)
        for pp in range(2):
            p = 2 * u + pp
            for k in range(9):
                first = (pp * 9 + k) * 16
                for g in range(low, high + 1):
                    lanes = slice(128 * g, 128 * g + 128)
                    band_ref[u, first : first + 16, lanes] = spread(p, k, 4 + 4 * g)
                if u in (0, 1, 4, 5):
                    rim_ref[u if u < 2 else u - 2, first : first + 16, :] = spread(p, k, 0 if u < 2 else 16)


def core_of():
    return lax.axis_index("lon") % 2


def halves_of(ref):
    core = core_of()
    own = pl.multiple_of(core * 128, 128)
    other = pl.multiple_of(128 - core * 128, 128)
    return jnp.concatenate([ref[pl.ds(own, 128), :], ref[pl.ds(other, 128), :]], axis=0)


def own_kernel(ext_ref, band_ref, feat_ref, y_ref, sums_ref, part_ref):
    for u in range(6):
        low, high = groups(u)
        band = band_ref[u, :, 128 * low : 128 * high + 128]
        for t in range(3):
            window = ext_ref[4 * low : 4 * high + 4, 16 * t : 16 * t + WIN, :].reshape(-1, 256)
            rows = jnp.dot(band, window, preferred_element_type=F32)
            if u in (2, 3):
                rows = rows.astype(BF16)
            for pp in range(2):
                start = (2 * u + pp) % 4 * WIDE + 16 * t
                for k in range(9):
                    first = (pp * 9 + k) * 16
                    if u in (2, 3):
                        y_ref[k, start : start + 16, :] = rows[first : first + 16]
            if u not in (2, 3):
                sums_ref[u if u < 2 else u - 2, t] = rows
    feat = halves_of(feat_ref)
    for k in range(9):
        part_ref[k] = jnp.dot(feat, y_ref[k], preferred_element_type=F32)


def edge_kernel(even_ref, odd_ref, rim_ref, sums_ref, part_ref, feat_ref, y_ref, send_ref):
    upper = lax.axis_index("lat") % 2 == 0
    for half in range(2):
        block = jnp.where(upper, odd_ref[...], even_ref[...])
        if half:
            block = jnp.where(upper, even_ref[...], odd_ref[...])
        for v in (2 * half, 2 * half + 1):
            rim = rim_ref[v]
            for t in range(3):
                window = block[:, 16 * t : 16 * t + WIN, :].reshape(-1, 256)
                rows = sums_ref[v, t] + jnp.dot(rim, window, preferred_element_type=F32)
                rows = rows.astype(BF16)
                for pp in range(2):
                    start = (2 * v + pp) * WIDE + 16 * t
                    for k in range(9):
                        first = (pp * 9 + k) * 16
                        y_ref[k, start : start + 16, :] = rows[first : first + 16]
    other = feat_ref[pl.ds(pl.multiple_of(128 - core_of() * 128, 128), 128), :]
    for k in range(9):
        part = part_ref[k, 128:] + jnp.dot(other, y_ref[k], preferred_element_type=F32)
        send_ref[k] = part.astype(BF16)


def keep_kernel(y_ref, part_ref, feat_ref, keep_ref):
    own = feat_ref[pl.ds(pl.multiple_of(core_of() * 128, 128), 128), :]
    for k in range(9):
        keep_ref[k] = part_ref[k, :128] + jnp.dot(own, y_ref[k], preferred_element_type=F32)


def input_kernel(middle_ref, edge_ref, w_ref, out_ref):
    def mixed(ref, rows):
        total = jnp.zeros((rows * WIDE, 256), F32)
        for k in range(9):
            total += lax.dot_general(
                ref[k], w_ref[k], (((1,), (1,)), ((), ())), preferred_element_type=F32
            )
        return total.reshape(rows, WIDE, 256)[:, :45].astype(BF16)

    out_ref[4:8] = mixed(middle_ref, 4)
    edge = mixed(edge_ref, 8)
    out_ref[:4] = edge[:4]
    out_ref[8:] = edge[4:]


def split_kernel(keep_ref, got_ref, out_ref):
    for i in range(16):
        rows, cols = slice(i // 2 * 16, i // 2 * 16 + 16), slice(i % 2 * 128, i % 2 * 128 + 128)
        part = keep_ref[:, rows, cols] + got_ref[:, rows, cols].astype(F32)
        j = i // 2 * 4 + i % 2
        out_ref[j] = part[:, :8].astype(BF16)
        out_ref[j + 2] = part[:, 8:].astype(BF16)


def sum_kernel(got_ref, out_ref):
    total = got_ref[0].astype(F32)
    for j in range(1, 32):
        total = total + got_ref[j].astype(F32)
    out_ref[...] = total.astype(BF16)


def join_kernel(scale, other, blocks_ref, *refs):
    out_ref, half_ref, sems = refs[-3:]
    start = pl.multiple_of((core_of() ^ other) * 128, 128)
    copies = []
    for part in range(2):
        for j in range(16 * part, 16 * part + 16):
            rows, cols = slice(j // 2 * 8, j // 2 * 8 + 8), slice(j % 2 * 128, j % 2 * 128 + 128)
            half_ref[:, rows, cols] = blocks_ref[j].astype(F32) * scale
        target = out_ref.at[:, pl.ds(pl.multiple_of(start + 64 * part, 64), 64), :]
        copies.append(pltpu.make_async_copy(half_ref.at[:, 64 * part : 64 * part + 64, :], target, sems.at[part]))
        copies[part].start()
    for copy in copies:
        copy.wait()


def call(kernel, outs, specs, *args, out_spec=None, scratch=(), aliases=None, **cost):
    estimate = pl.CostEstimate(transcendentals=0, **cost) if cost else None
    out_spec = out_spec or pl.BlockSpec(memory_space=pltpu.VMEM)
    return pl.pallas_call(
        kernel,
        out_shape=outs,
        in_specs=specs,
        out_specs=jax.tree.map(lambda _: out_spec, outs),
        scratch_shapes=scratch,
        input_output_aliases=aliases or {},
        compiler_params=PARAMS,
        cost_estimate=estimate,
    )(*args)


def shape(dims, dtype):
    return jax.ShapeDtypeStruct(dims, dtype)


def local(features, cotangent, weights, quad_weights, reach_table):
    slab = shape((12, 8, 256), BF16)
    even, odd, ext = call(
        rim_kernel, (slab, slab, shape((12, 64, 256), BF16)), whole(1), cotangent,
        flops=2 * 10**10, bytes_accessed=10**6,
    )
    even = lax.ppermute(even, "lon", chain(0, True))
    odd = lax.ppermute(odd, "lon", chain(1, True))
    band, rims, feat, feat_edge = call(
        band_kernel,
        (
            shape((6, 288, 12 * WIN), BF16), shape((4, 288, 4 * WIN), BF16),
            shape((256, 4 * WIDE), BF16), shape((256, 8 * WIDE), BF16),
        ),
        whole(3), quad_weights.transpose(0, 2, 3, 1), reach_table.T, features,
        scratch=[
            pltpu.VMEM((12, WIDE, 256), BF16), pltpu.VMEM((84 * WIN, 192), BF16), pltpu.VMEM((84, 32, 128), F32),
        ],
    )
    even, odd, band = lax.optimization_barrier((even, odd, band))
    rim = shape((4, 64, 256), BF16)
    ext, even, odd = call(
        extend_kernel, (shape((12, 64, 256), BF16), rim, rim), whole(3), ext, even, odd
    )
    even = lax.ppermute(even, "lat", chain(0, False))
    odd = lax.ppermute(odd, "lat", chain(1, False))
    y, sums, part = call(
        own_kernel,
        (shape((9, 4 * WIDE, 256), BF16), shape((4, 3, 288, 256), F32), shape((9, 256, 256), F32)),
        whole(3), ext, band, feat, flops=10**6, bytes_accessed=10**6,
    )
    even, odd, part = lax.optimization_barrier((even, odd, part))
    halves, blocks = (9, 128, 256), (32, 9, 8, 128)
    y_edge, out = call(
        edge_kernel, (shape((9, 8 * WIDE, 256), BF16), shape(halves, BF16)), whole(6),
        even, odd, rims, sums, part, feat_edge,
    )
    got = send(out, CORE)
    keep = call(
        keep_kernel, shape(halves, F32), whole(3), y_edge, part, feat_edge,
        flops=10**9, bytes_accessed=4 * 10**6,
    )
    got = trade(call(split_kernel, shape(blocks, BF16), whole(2), keep, got))
    mine = call(sum_kernel, shape(blocks[1:], BF16), whole(1), got)
    mine, y, y_edge = lax.optimization_barrier((mine, y, y_edge))
    gots = [send(mine, r).astype(F32) for r in QUAD]
    total = (mine.astype(F32) + gots[0]) + (gots[1] + gots[2])
    grad_input = call(
        input_kernel, shape((12, 45, 256), BF16), whole(3), y, y_edge, weights,
        flops=2 * 10**9, bytes_accessed=4 * 10**6,
    )
    total, grad_input = lax.optimization_barrier((total, grad_input))
    own = trade(jnp.broadcast_to(total.astype(BF16), blocks))
    got = send(own, CORE)
    scale = 1.0 / math.sqrt(192 * 720)
    scratch = [pltpu.VMEM(halves, F32), pltpu.SemaphoreType.DMA((2,))]
    full = shape((9, 256, 256), F32)
    grad_weight = call(
        functools.partial(join_kernel, scale, 0), full, whole(1), own,
        out_spec=ANY, scratch=scratch, flops=10**6, bytes_accessed=2 * 10**6,
    )
    grad_weight = call(
        functools.partial(join_kernel, scale, 1), full, whole(1) + [ANY], got, grad_weight,
        out_spec=ANY, scratch=scratch, aliases={1: 0}, flops=10**6, bytes_accessed=2 * 10**6,
    )
    return grad_input, grad_weight


def solution(mesh):
    return jax.shard_map(
        local,
        mesh=mesh,
        in_specs=(P("lat", "lon", None), P("lat", "lon", None), P(), P(), P()),
        out_specs=(P("lat", "lon", None), P()),
        check_vma=False,
    )
```
